512 devices in a mesh: row: 16 (over y_lo, x, core), col: 32 (over z, y_hi).
Axes of the slice: x: 4, y: 4 (y_hi: 2, y_lo: 2; y = y_hi * 2 + y_lo), z: 16, core: 2. Of those that a mesh axis runs over, the one named last changes fastest.
Arguments:
- projected: bfloat16 [3, 2048, 16, 32, 128], P(None, None, 'row', 'col'), may hold values from -6 to 6
- short_taps: float32 [3, 2048, 3], replicated, may hold values from -3 to 3
- long_filter: bfloat16 [2048, 16, 32, 128], P(None, 'row', 'col'), may hold values from -6 to 6
- skip_gain: float32 [2048], replicated, may hold values from 0.5 to 1.5
- cotangent: bfloat16 [2048, 16, 32, 128], P(None, 'row', 'col'), may hold values from -6 to 6
Outputs:
- filter_grad: bfloat16 [2048, 16, 32, 128], P(None, 'row', 'col')
- projected_grad: bfloat16 [3, 2048, 16, 32, 128], P(None, None, 'row', 'col')
The draws below stay inside these ranges and needn't reach their ends.
All inputs are finite; a program needn't handle non-finite values.
Results may differ from the reference program's by a relative error of at most 0.0049.
Values may be sent and summed in bfloat16 or wider, within the bound.
A program may use at most 64 MiB of HBM per device.

```python
import jax
import jax.numpy as jnp
from jax import lax

CHANNELS = 2048
TURNS = 128
GRID_ROWS = 16
GRID_COLS = 32
SEQ_LEN = 65536


def shard_levels(key, extent, split, smallest, largest):
    factor_of = 1.0
    for position, shards_of in split:
        heights = jax.random.uniform(jax.random.fold_in(jax.random.fold_in(key, 6), position), (shards_of,), jnp.float32, smallest / len(split), largest / len(split))
        factor_of = factor_of * jnp.repeat(jnp.exp(heights), extent[position] // shards_of).reshape((-1,) + (1,) * (len(extent) - 1 - position))
    return factor_of


def scatter_about(rng, shape, spread, reach, split=(), held_as=jnp.bfloat16):
    entries = spread * jax.random.normal(rng, shape, jnp.float32)
    if split:
        entries = entries * shard_levels(rng, shape, split, -0.22, 0.18)
    return jnp.clip(entries, -reach, reach).astype(held_as)


def setup_inputs(seed: int = 0) -> dict:
    splits = jax.random.split(jax.random.key(seed), 6)
    projected = scatter_about(splits[0], (3, CHANNELS, GRID_ROWS, GRID_COLS, TURNS), 1.0, 6.0, ((2, 16), (3, 32)))
    short_taps = scatter_about(splits[1], (3, CHANNELS, 3), 0.6, 3.0, (), jnp.float32)
    long_filter = scatter_about(splits[2], (CHANNELS, GRID_ROWS, GRID_COLS, TURNS), 1.0, 6.0, ((1, 16), (2, 32)))
    skip_gain = jnp.clip(jax.random.uniform(splits[3], (CHANNELS,), jnp.float32, 0.5, 1.5), 0.5, 1.5)
    cotangent = scatter_about(splits[4], (CHANNELS, GRID_ROWS, GRID_COLS, TURNS), 1.0, 6.0, ((1, 16), (2, 32)))
    return dict(projected=projected, short_taps=short_taps, long_filter=long_filter, skip_gain=skip_gain, cotangent=cotangent)


def to_sequence(grid_values):
    moved = jnp.moveaxis(grid_values, -1, -3)
    return moved.reshape(moved.shape[:-3] + (SEQ_LEN,))


def to_grid(line_values):
    shaped = line_values.reshape(line_values.shape[:-1] + (TURNS, GRID_ROWS, GRID_COLS))
    return jnp.moveaxis(shaped, -3, -1)


def one_channel(pieces):
    projected_grid, taps_row, filter_grid, gain_value, seed_grid = pieces
    projected_line = to_sequence(projected_grid.astype(jnp.float32))
    padded = jnp.pad(projected_line, ((0, 0), (2, 0)))
    features = (taps_row[:, 0:1] * projected_line + taps_row[:, 1:2] * padded[:, 1:-1]
                + taps_row[:, 2:3] * padded[:, :-2])
    query_line = features[0]
    keys_line = features[1]
    values_line = features[2]
    gated_signal = keys_line * values_line
    filter_line = to_sequence(filter_grid.astype(jnp.float32))
    seed_line = to_sequence(seed_grid.astype(jnp.float32))
    weighted = query_line * seed_line
    filter_factor = SEQ_LEN ** -0.5
    gated_spectrum = jnp.fft.fft(gated_signal)
    filter_spectrum = jnp.fft.fft(filter_line)
    weighted_spectrum = jnp.fft.fft(weighted)
    convolved = jnp.fft.ifft(gated_spectrum * filter_spectrum).real * filter_factor
    filter_grad = (jnp.fft.ifft(weighted_spectrum * jnp.conj(gated_spectrum)).real * filter_factor).astype(jnp.bfloat16)
    gated_grad = jnp.fft.ifft(weighted_spectrum * jnp.conj(filter_spectrum)).real * filter_factor + gain_value * weighted
    mixed_inner = convolved + gain_value * gated_signal
    feature_grad = jnp.stack([seed_line * mixed_inner, gated_grad * values_line, gated_grad * keys_line]).astype(jnp.bfloat16)
    feature_back = lax.optimization_barrier(feature_grad).astype(jnp.float32)
    padded_ahead = jnp.pad(feature_back, ((0, 0), (0, 2)))
    projected_grad = (taps_row[:, 0:1] * feature_back + taps_row[:, 1:2] * padded_ahead[:, 1:-1]
                      + taps_row[:, 2:3] * padded_ahead[:, 2:]).astype(jnp.bfloat16)
    return to_grid(filter_grad), to_grid(projected_grad)


def reference(projected, short_taps, long_filter, skip_gain, cotangent):
    filter_grad, projected_grad = lax.map(
        one_channel,
        (jnp.moveaxis(projected, 1, 0), jnp.moveaxis(short_taps, 1, 0), long_filter, skip_gain, cotangent))
    return filter_grad, jnp.moveaxis(projected_grad, 0, 1)
```

```python
import math

import jax
import jax.numpy as jnp
import numpy as np
from jax import lax
from jax.sharding import PartitionSpec as P


def tables(turns, slots):
    length = turns * slots
    half = turns // 2 + 1
    k = np.arange(half)
    s = np.arange(turns)
    r = np.arange(slots)
    ang = 2.0 * math.pi * (np.outer(k, s) % turns) / turns
    first = np.concatenate([np.cos(ang), -np.sin(ang)], axis=0)
    weight = np.where((k == 0) | (k == turns // 2), 1.0, 2.0)[:, None]
    scale = 1.0 / length * length**-0.5
    last = np.concatenate([weight * np.cos(ang), weight * np.sin(ang)], axis=0) * scale
    ang = 2.0 * math.pi * np.outer(k, r) / length
    twist = (np.cos(ang).astype(np.float32), np.sin(ang).astype(np.float32))
    ang = 2.0 * math.pi * (np.outer(r, r) % slots) / slots
    c, sn = np.cos(ang), np.sin(ang)
    block = np.concatenate(
        [np.concatenate([c, -sn], axis=1), np.concatenate([sn, c], axis=1)], axis=0
    )
    return first, last, twist, block


def two(table):
    high = table.astype(np.float32).astype(jnp.bfloat16)
    low = (table - high.astype(np.float64)).astype(np.float32).astype(jnp.bfloat16)
    return jnp.asarray(high), jnp.asarray(low)


def parts_of(values):
    high = values.astype(jnp.bfloat16)
    low = (values - high.astype(jnp.float32)).astype(jnp.bfloat16)
    return high, low


def product(form, values, table):
    high, low = parts_of(values)
    t_high, t_low = table

    def one(left, right):
        return jnp.einsum(form, left, right, preferred_element_type=jnp.float32)

    return one(high, t_high) + (one(low, t_high) + one(high, t_low))


def earlier(lines):
    wrapped = jnp.pad(lines[..., -1:, :-1], [(0, 0)] * (lines.ndim - 1) + [(1, 0)])
    return jnp.concatenate([wrapped, lines[..., :-1, :]], axis=-2)


def later(lines):
    wrapped = jnp.pad(lines[..., :1, 1:], [(0, 0)] * (lines.ndim - 1) + [(0, 1)])
    return jnp.concatenate([lines[..., 1:, :], wrapped], axis=-2)


def owner(lines, taps, gain):
    slots, turns = lines.shape[-2:]
    half = turns // 2 + 1
    first, last, twist, block = tables(turns, slots)
    first, last, block = two(first), two(last), two(block)
    cos_t, sin_t = jnp.asarray(twist[0]), jnp.asarray(twist[1])
    taps = taps[..., None, None]
    gain = gain[:, None, None]
    lines = lines.astype(jnp.float32)
    raw = lines[:3]
    once = earlier(raw)
    features = taps[:, :, 0] * raw + taps[:, :, 1] * once + taps[:, :, 2] * earlier(once)
    query, keys, values = features[0], features[1], features[2]
    filt, seed = lines[3], lines[4]
    gated = keys * values
    weighted = query * seed
    spectra = product("fnrs,ks->fnkr", jnp.stack([gated, filt, weighted]), first)
    re, im = spectra[:, :, :half], spectra[:, :, half:]
    both = jnp.concatenate([re * cos_t + im * sin_t, im * cos_t - re * sin_t], axis=-1)
    both = product("fnkr,rq->fnkq", both, block)
    re, im = both[..., :slots], both[..., slots:]
    gr, fr, wr = re[0], re[1], re[2]
    gi, fi, wi = im[0], im[1], im[2]
    out_re = jnp.stack([gr * fr - gi * fi, wr * fr + wi * fi, wr * gr + wi * gi])
    neg_im = jnp.stack([-gr * fi - gi * fr, wr * fi - wi * fr, wr * gi - wi * gr])
    both = product("fnkq,qr->fnkr", jnp.concatenate([out_re, neg_im], axis=-1), block)
    re, nim = both[..., :slots], both[..., slots:]
    e_re = re * cos_t + nim * sin_t
    e_nim = nim * cos_t - re * sin_t
    lines = product("fnkr,ks->fnrs", jnp.concatenate([e_re, e_nim], axis=2), last)
    conv, back, filter_grad = lines[0], lines[1], lines[2]
    gated_grad = back + gain * weighted
    mixed = conv + gain * gated
    grads = jnp.stack([seed * mixed, gated_grad * values, gated_grad * keys]).astype(jnp.bfloat16)
    grads = lax.optimization_barrier(grads).astype(jnp.float32)
    once = later(grads)
    projected = taps[:, :, 0] * grads + taps[:, :, 1] * once + taps[:, :, 2] * later(once)
    return jnp.concatenate([projected, filter_grad[None]]).astype(jnp.bfloat16)


def on_device(projected, short_taps, long_filter, skip_gain, cotangent):
    channels = short_taps.shape[1]
    turns = projected.shape[-1]
    rows = lax.axis_size("row")
    cols = lax.axis_size("col")
    slots = rows * cols
    each = channels // slots
    rank = lax.axis_index("row") * cols + lax.axis_index("col")
    stacked = jnp.concatenate(
        [
            projected.reshape(3, channels, turns),
            long_filter.reshape(1, channels, turns),
            cotangent.reshape(1, channels, turns),
        ]
    )
    outgoing = stacked.reshape(5, rows, cols, each, 1, 1, turns)
    arrived = lax.all_to_all(
        lax.all_to_all(outgoing, "row", split_axis=1, concat_axis=4, tiled=True),
        "col",
        split_axis=2,
        concat_axis=5,
        tiled=True,
    )
    taps = lax.dynamic_slice_in_dim(short_taps, rank * each, each, 1)
    gain = lax.dynamic_slice_in_dim(skip_gain, rank * each, each, 0)
    results = owner(arrived.reshape(5, each, slots, turns), taps, gain)
    returned = lax.all_to_all(
        lax.all_to_all(
            results.reshape(4, 1, 1, each, rows, cols, turns),
            "col",
            split_axis=5,
            concat_axis=2,
            tiled=True,
        ),
        "row",
        split_axis=4,
        concat_axis=1,
        tiled=True,
    )
    lines = returned.reshape(4, channels, turns)
    return (
        lines[3].reshape(channels, 1, 1, turns),
        lines[:3].reshape(3, channels, 1, 1, turns),
    )


def solution(mesh):
    in_specs = (
        P(None, None, "row", "col", None),
        P(),
        P(None, "row", "col", None),
        P(),
        P(None, "row", "col", None),
    )
    out_specs = (P(None, "row", "col", None), P(None, None, "row", "col", None))
    return jax.shard_map(
        on_device, mesh=mesh, in_specs=in_specs, out_specs=out_specs, check_vma=False
    )
```

```python
import functools
import math

import jax
import jax.numpy as jnp
import numpy as np
from jax import lax
from jax.experimental import pallas as pl
from jax.experimental.pallas import tpu as pltpu
from jax.sharding import PartitionSpec as P

MESH = pl.DeviceIdType.MESH
BF16 = jnp.bfloat16
F32 = jnp.float32
PAD = 80


def two(table):
    high = table.astype(np.float32).astype(BF16)
    low = (table - high.astype(np.float64)).astype(np.float32).astype(BF16)
    return np.stack([high, low])


def tables(turns, planes, depth):
    slots = planes * depth
    length = turns * slots
    half = turns // 2 + 1
    z, g = np.meshgrid(np.arange(depth), np.arange(planes), indexing="ij")
    r = ((g // 2) * 2 * depth + z * 2 + g % 2).reshape(-1)
    k = np.arange(half)
    angles = 2.0 * math.pi * (np.outer(k, np.arange(turns)) % turns) / turns
    weight = np.where((k == 0) | (k == turns // 2), 1.0, 2.0)[:, None]
    scale = 1.0 / length * length**-0.5

    def padded(table):
        return np.pad(table, [(0, PAD - half), (0, 0)])

    cosine, sine = padded(np.cos(angles)), padded(np.sin(angles))
    first = np.concatenate([cosine, -sine])
    weight = padded(weight) * scale
    last = np.concatenate([weight * cosine, weight * sine]).T
    angles = 2.0 * math.pi * np.outer(k, r) / length
    twist = np.stack([padded(np.cos(angles)), padded(np.sin(angles))]).astype(np.float32)
    angles = 2.0 * math.pi * (np.outer(r, r) % slots) / slots
    cosine, sine = np.cos(angles), np.sin(angles)
    block = np.block([[cosine, -sine], [sine, cosine]])
    return two(first), two(last), twist, two(block)


def split(values):
    high = values.astype(BF16)
    return high, (values - high.astype(F32)).astype(BF16)


def dot(left, right):
    return jnp.dot(left, right, preferred_element_type=F32)


def dot_t(left, right):
    return lax.dot_general(left, right, (((1,), (1,)), ((), ())), preferred_element_type=F32)


def kernel(
    planes,
    depth,
    scalars,
    projected,
    filt,
    cotangent,
    first_hbm,
    last_hbm,
    twist_hbm,
    block_hbm,
    filter_out,
    projected_out,
    held,
    arrived1,
    leaving2,
    arrived2,
    leaving3,
    arrived3,
    leaving4,
    arrived4,
    first,
    last,
    twist,
    block,
    flat,
    lines,
    spectra,
    factors,
    load_sem,
    table_sem,
    send_sem,
    recv_sem,
    out_sem,
):
    chunks = held.shape[0]
    turns = held.shape[-1]
    slots = planes * depth
    row = lax.axis_index("row")
    col = lax.axis_index("col")
    z = col // 2
    g = row * 2 + col % 2

    def at_plane(step):
        peer = lax.rem(g + step, planes)
        return peer, (peer // 2, z * 2 + lax.rem(peer, 2))

    def at_depth(step):
        away = (1 - 2 * lax.rem(step, 2)) * (step // 2 + 1)
        peer = lax.rem(z + away + depth, depth)
        return peer, (row, peer * 2 + lax.rem(col, 2))

    def await_bytes(ref, sem):
        pltpu.make_async_copy(ref, ref, sem).wait()

    def load_copies(j):
        rows = pl.ds(j * slots, slots)
        return (
            pltpu.make_async_copy(
                projected.at[:, rows], held.at[j, pl.ds(0, 3)], load_sem.at[j, 0]
            ),
            pltpu.make_async_copy(filt.at[rows], held.at[j, 3], load_sem.at[j, 1]),
            pltpu.make_async_copy(cotangent.at[rows], held.at[j, 4], load_sem.at[j, 2]),
        )

    def table_copies():
        return (
            pltpu.make_async_copy(first_hbm, first, table_sem.at[0]),
            pltpu.make_async_copy(last_hbm, last, table_sem.at[1]),
            pltpu.make_async_copy(twist_hbm, twist, table_sem.at[2]),
            pltpu.make_async_copy(block_hbm, block, table_sem.at[3]),
        )

    def out_copies(j):
        rows = pl.ds(j * slots, slots)
        return (
            pltpu.make_async_copy(
                arrived4.at[j, pl.ds(0, 3)], projected_out.at[:, rows], out_sem.at[j, 0]
            ),
            pltpu.make_async_copy(arrived4.at[j, 3], filter_out.at[rows], out_sem.at[j, 1]),
        )

    def loop(count, body):
        lax.fori_loop(0, count, lambda i, carry: (body(i), carry)[1], 0)

    for j in range(chunks):
        for copy in load_copies(j):
            copy.start()
    for copy in table_copies():
        copy.start()

    barrier = pltpu.get_barrier_semaphore()

    def greet_plane(i):
        _, device = at_plane(i + 1)
        pl.semaphore_signal(barrier, inc=1, device_id=device, device_id_type=MESH)

    def greet_depth(i):
        _, device = at_depth(i)
        pl.semaphore_signal(barrier, inc=1, device_id=device, device_id_type=MESH)

    loop(planes - 1, greet_plane)
    loop(depth - 1, greet_depth)
    pl.semaphore_wait(barrier, planes + depth - 2)

    def send_all(phase, j, count, at, own, source, target):
        pltpu.make_async_copy(source(own), target(own), recv_sem.at[phase, j]).start()

        def one(i):
            peer, device = at(i)
            pltpu.make_async_remote_copy(
                src_ref=source(peer),
                dst_ref=target(own),
                send_sem=send_sem.at[phase, j],
                recv_sem=recv_sem.at[phase, j],
                device_id=device,
                device_id_type=MESH,
            ).start()

        loop(count - 1, one)

    def next_plane(i):
        return at_plane(i + 1)

    def enter(j):
        for copy in load_copies(j):
            copy.wait()
        send_all(
            0,
            j,
            planes,
            next_plane,
            g,
            lambda peer: held.at[j, :, pl.ds(pl.multiple_of(peer * depth, depth), depth)],
            lambda own: arrived1.at[j, own],
        )

    loop(chunks, enter)

    def pass_on(j):
        await_bytes(arrived1.at[j], recv_sem.at[0, j])

        def sort(i):
            flat[...] = arrived1[j, :, i].astype(F32).reshape(slots, turns)
            for peer in range(depth):
                leaving2[j, peer, i] = flat[pl.ds(peer, planes, stride=depth), :].astype(BF16)

        loop(5, sort)
        send_all(
            1,
            j,
            depth,
            at_depth,
            z,
            lambda peer: leaving2.at[j, peer],
            lambda own: arrived2.at[j, own],
        )

    loop(chunks, pass_on)

    for copy in table_copies():
        copy.wait()

    row_of = lax.broadcasted_iota(jnp.int32, (slots, turns), 0)
    odd = lax.rem(row_of, 2) == 1
    edge_row = lax.broadcasted_iota(jnp.int32, (planes, turns), 0)
    edge_lane = lax.broadcasted_iota(jnp.int32, (planes, turns), 1)

    def earlier(now):
        edge = pltpu.roll(now[slots - planes :], 2, 0)
        wrapped = jnp.where(edge_lane == 0, 0.0, pltpu.roll(edge, 1, 1))
        edge = jnp.where(edge_row < 2, wrapped, edge)
        second = jnp.concatenate([edge, now[: slots - planes]], axis=0)
        return jnp.where(odd, pltpu.roll(now, 1, 0), pltpu.roll(second, slots - 1, 0)), second

    def later(now):
        edge = pltpu.roll(now[:planes], planes - 2, 0)
        wrapped = jnp.where(edge_lane == turns - 1, 0.0, pltpu.roll(edge, turns - 1, 1))
        edge = jnp.where(edge_row >= planes - 2, wrapped, edge)
        second = jnp.concatenate([now[planes:], edge], axis=0)
        return jnp.where(odd, pltpu.roll(second, 1, 0), pltpu.roll(now, slots - 1, 0)), second

    def transform():
        width = min(256, 2 * slots)

        def columns(i):
            at = pl.ds(pl.multiple_of(i * width, width), width)
            high, low = factors[0], factors[1]
            spectra[:, at] = dot(high, block[0, :, at]) + (
                dot(low, block[0, :, at]) + dot(high, block[1, :, at])
            )

        loop(2 * slots // width, columns)

    def put(i, real, imag):
        rows = pl.ds(i * PAD, PAD)
        for side, part in ((0, real), (slots, imag)):
            high, low = split(part)
            factors[0, rows, pl.ds(side, slots)] = high
            factors[1, rows, pl.ds(side, slots)] = low

    def get(i):
        rows = pl.ds(i * PAD, PAD)
        return spectra[rows, pl.ds(0, slots)], spectra[rows, pl.ds(slots, slots)]

    def own_channel(j):
        await_bytes(arrived2.at[j], recv_sem.at[1, j])

        def line(i):
            return arrived2[j, :, i].astype(F32).reshape(slots, turns)

        def feature(i):
            now = line(i)
            first_back, second_back = earlier(now)
            return (
                scalars[j * 10 + i * 3] * now
                + scalars[j * 10 + i * 3 + 1] * first_back
                + scalars[j * 10 + i * 3 + 2] * second_back
            )

        lines[0] = feature(1)
        lines[1] = feature(2)
        lines[2] = lines[0] * lines[1]
        lines[3] = line(3)
        lines[4] = feature(0) * line(4)

        def spectrum(i):
            high, low = split(lines[2 + i])
            turned = dot_t(first[0], high) + (dot_t(first[0], low) + dot_t(first[1], high))
            real, imag = turned[:PAD], turned[PAD:]
            put(i, real * twist[0] + imag * twist[1], imag * twist[0] - real * twist[1])

        for i in range(3):
            spectrum(i)
        transform()
        gated_re, gated_im = get(0)
        filt_re, filt_im = get(1)
        put(
            0,
            gated_re * filt_re - gated_im * filt_im,
            -(gated_re * filt_im) - gated_im * filt_re,
        )
        gated_re, gated_im = get(0)
        filt_re, filt_im = get(1)
        side_re, side_im = get(2)
        put(
            1,
            side_re * filt_re + side_im * filt_im,
            side_re * filt_im - side_im * filt_re,
        )
        put(
            2,
            side_re * gated_re + side_im * gated_im,
            side_re * gated_im - side_im * gated_re,
        )
        transform()

        def back(i):
            real, imag = get(i)
            turned = jnp.concatenate(
                [real * twist[0] + imag * twist[1], imag * twist[0] - real * twist[1]], axis=0
            )
            high, low = split(turned)
            result = dot(last[0], high) + (dot(last[0], low) + dot(last[1], high))
            return jnp.transpose(result)

        gain = scalars[j * 10 + 9]
        lines[2] = back(0) + gain * lines[2]
        lines[4] = back(1) + gain * lines[4]
        leaving3[j, :, 3] = back(2).astype(BF16).reshape(depth, planes, turns)

        def leave(i, grad):
            now = grad.astype(BF16).astype(F32)
            first_next, second_next = later(now)
            total = (
                scalars[j * 10 + i * 3] * now
                + scalars[j * 10 + i * 3 + 1] * first_next
                + scalars[j * 10 + i * 3 + 2] * second_next
            )
            leaving3[j, :, i] = total.astype(BF16).reshape(depth, planes, turns)

        leave(0, line(4) * lines[2])
        leave(1, lines[4] * lines[1])
        leave(2, lines[4] * lines[0])
        send_all(
            2,
            j,
            depth,
            at_depth,
            z,
            lambda peer: leaving3.at[j, peer],
            lambda own: arrived3.at[j, own],
        )

    loop(chunks, own_channel)

    def hand_back(j):
        await_bytes(arrived3.at[j], recv_sem.at[2, j])

        def sort(i):
            flat[...] = arrived3[j, :, i].astype(F32).reshape(slots, turns)
            for peer in range(planes):
                leaving4[j, peer, i] = flat[pl.ds(peer, depth, stride=planes), :].astype(BF16)

        loop(4, sort)
        send_all(
            3,
            j,
            planes,
            next_plane,
            g,
            lambda peer: leaving4.at[j, peer],
            lambda own: arrived4.at[j, :, pl.ds(pl.multiple_of(own * depth, depth), depth)],
        )

    loop(chunks, hand_back)

    def finish(j):
        await_bytes(arrived4.at[j], recv_sem.at[3, j])
        for copy in out_copies(j):
            copy.start()

    loop(chunks, finish)

    def close(j):
        for copy in out_copies(j):
            copy.wait()
        await_bytes(held.at[j, :, pl.ds(0, (planes - 1) * depth)], send_sem.at[0, j])
        await_bytes(leaving2.at[j, pl.ds(0, depth - 1)], send_sem.at[1, j])
        await_bytes(leaving3.at[j, pl.ds(0, depth - 1)], send_sem.at[2, j])
        await_bytes(leaving4.at[j, pl.ds(0, planes - 1)], send_sem.at[3, j])

    loop(chunks, close)


def on_device(projected, short_taps, long_filter, skip_gain, cotangent):
    channels = short_taps.shape[1]
    turns = projected.shape[-1]
    rows = lax.axis_size("row")
    depth = lax.axis_size("col") // 2
    planes = rows * 2
    slots = planes * depth
    chunks = channels // slots
    col = lax.axis_index("col")
    place = (lax.axis_index("row") * 2 + col % 2) * depth + col // 2
    taps = lax.dynamic_slice_in_dim(
        short_taps.reshape(3, chunks, slots, 3), place, 1, 2
    ).reshape(3, chunks, 3)
    gain = lax.dynamic_slice_in_dim(skip_gain.reshape(chunks, slots), place, 1, 1)
    scalars = jnp.concatenate(
        [jnp.swapaxes(taps, 0, 1).reshape(chunks, 9), gain], axis=1
    ).reshape(-1)
    made = [jnp.asarray(t) for t in tables(turns, planes, depth)]
    anywhere = pl.BlockSpec(memory_space=pl.ANY)

    def vmem(*shape, dtype=BF16):
        return pltpu.VMEM(shape, dtype)

    filter_grad, projected_grad = pl.pallas_call(
        functools.partial(kernel, planes, depth),
        out_shape=(
            jax.ShapeDtypeStruct((channels, turns), BF16),
            jax.ShapeDtypeStruct((3, channels, turns), BF16),
        ),
        in_specs=[pl.BlockSpec(memory_space=pltpu.SMEM)] + [anywhere] * 7,
        out_specs=(anywhere, anywhere),
        scratch_shapes=[
            vmem(chunks, 5, slots, turns),
            vmem(chunks, planes, 5, depth, turns),
            vmem(chunks, depth, 5, planes, turns),
            vmem(chunks, depth, 5, planes, turns),
            vmem(chunks, depth, 4, planes, turns),
            vmem(chunks, depth, 4, planes, turns),
            vmem(chunks, planes, 4, depth, turns),
            vmem(chunks, 4, slots, turns),
            *[pltpu.VMEM(t.shape, t.dtype) for t in made],
            vmem(slots, turns, dtype=F32),
            vmem(5, slots, turns, dtype=F32),
            vmem(3 * PAD, 2 * slots, dtype=F32),
            vmem(2, 3 * PAD, 2 * slots),
            pltpu.SemaphoreType.DMA((chunks, 3)),
            pltpu.SemaphoreType.DMA((4,)),
            pltpu.SemaphoreType.DMA((4, chunks)),
            pltpu.SemaphoreType.DMA((4, chunks)),
            pltpu.SemaphoreType.DMA((chunks, 2)),
        ],
        compiler_params=pltpu.CompilerParams(
            collective_id=0, has_side_effects=True, vmem_limit_bytes=56 << 20
        ),
    )(
        scalars,
        projected.reshape(3, channels, turns),
        long_filter.reshape(channels, turns),
        cotangent.reshape(channels, turns),
        *made,
    )
    return (
        filter_grad.reshape(channels, 1, 1, turns),
        projected_grad.reshape(3, channels, 1, 1, turns),
    )


def solution(mesh):
    in_specs = (
        P(None, None, "row", "col", None),
        P(),
        P(None, "row", "col", None),
        P(),
        P(None, "row", "col", None),
    )
    out_specs = (P(None, "row", "col", None), P(None, None, "row", "col", None))
    return jax.shard_map(
        on_device, mesh=mesh, in_specs=in_specs, out_specs=out_specs, check_vma=False
    )
```

```python
import functools
import math

import jax
import jax.numpy as jnp
import numpy as np
from jax import lax
from jax.experimental import pallas as pl
from jax.experimental.pallas import tpu as pltpu
from jax.sharding import PartitionSpec as P

MESH = pl.DeviceIdType.MESH
BF16 = jnp.bfloat16
F32 = jnp.float32
PAD = 80


def two(table):
    high = table.astype(np.float32).astype(BF16)
    low = (table - high.astype(np.float64)).astype(np.float32).astype(BF16)
    return np.stack([high, low])


def tables(turns, planes, depth):
    slots = planes * depth
    length = turns * slots
    half = turns // 2 + 1
    z, g = np.meshgrid(np.arange(depth), np.arange(planes), indexing="ij")
    r = ((g // 2) * 2 * depth + z * 2 + g % 2).reshape(-1)
    k = np.arange(half)
    angles = 2.0 * math.pi * (np.outer(k, np.arange(turns)) % turns) / turns
    weight = np.where((k == 0) | (k == turns // 2), 1.0, 2.0)[:, None]
    scale = 1.0 / length * length**-0.5

    def padded(table):
        return np.pad(table, [(0, PAD - half), (0, 0)])

    cosine, sine = padded(np.cos(angles)), padded(np.sin(angles))
    first = np.concatenate([cosine, -sine])
    weight = padded(weight) * scale
    last = np.concatenate([weight * cosine, weight * sine]).T
    angles = 2.0 * math.pi * np.outer(k, r) / length
    twist = np.stack([padded(np.cos(angles)), padded(np.sin(angles))]).astype(np.float32)
    angles = 2.0 * math.pi * (np.outer(r, r) % slots) / slots
    cosine, sine = np.cos(angles), np.sin(angles)
    block = np.block([[cosine, -sine], [sine, cosine]])
    return two(first), two(last), twist, two(block)


def split(values):
    high = values.astype(BF16)
    return high, (values - high.astype(F32)).astype(BF16)


def dot(left, right):
    return jnp.dot(left, right, preferred_element_type=F32)


def dot_t(left, right):
    return lax.dot_general(left, right, (((1,), (1,)), ((), ())), preferred_element_type=F32)


def kernel(
    planes,
    depth,
    taps_hbm,
    gains_hbm,
    projected,
    filt,
    cotangent,
    first_hbm,
    last_hbm,
    twist_hbm,
    block_hbm,
    filter_out,
    projected_out,
    held,
    own_in,
    leaving_in,
    arrived_in,
    own_out,
    leaving_out,
    arrived_out,
    returned,
    taps,
    gains,
    first,
    last,
    twist,
    block,
    flat,
    lines,
    spectra,
    factors,
    load_sem,
    table_sem,
    send_sem,
    recv_sem,
    out_sem,
):
    chunks = held.shape[0]
    turns = held.shape[-1]
    slots = planes * depth
    row = lax.axis_index("row")
    col = lax.axis_index("col")
    z = col // 2
    g = row * 2 + lax.rem(col, 2)

    def at_plane(step):
        peer = lax.rem(g + step + 1, planes)
        return peer, (peer // 2, z * 2 + lax.rem(peer, 2))

    def at_depth(step):
        away = (1 - 2 * lax.rem(step, 2)) * (step // 2 + 1)
        peer = lax.rem(z + away + depth, depth)
        return peer, (row, peer * 2 + lax.rem(col, 2))

    def await_bytes(ref, sem):
        pltpu.make_async_copy(ref, ref, sem).wait()

    def load_copies(j):
        rows = pl.ds(j * slots, slots)
        return (
            pltpu.make_async_copy(
                projected.at[:, rows], held.at[j, pl.ds(0, 3)], load_sem.at[j, 0]
            ),
            pltpu.make_async_copy(filt.at[rows], held.at[j, 3], load_sem.at[j, 1]),
            pltpu.make_async_copy(cotangent.at[rows], held.at[j, 4], load_sem.at[j, 2]),
        )

    def table_copies():
        pairs = (
            (taps_hbm, taps),
            (gains_hbm, gains),
            (first_hbm, first),
            (last_hbm, last),
            (twist_hbm, twist),
            (block_hbm, block),
        )
        return [
            pltpu.make_async_copy(source, target, table_sem.at[i])
            for i, (source, target) in enumerate(pairs)
        ]

    def out_copies(j):
        rows = pl.ds(j * slots, slots)
        return (
            pltpu.make_async_copy(
                returned.at[j, pl.ds(0, 3)], projected_out.at[:, rows], out_sem.at[j, 0]
            ),
            pltpu.make_async_copy(returned.at[j, 3], filter_out.at[rows], out_sem.at[j, 1]),
        )

    def loop(count, body):
        lax.fori_loop(0, count, lambda i, carry: (body(i), carry)[1], 0)

    for j in range(chunks):
        for copy in load_copies(j):
            copy.start()
    for copy in table_copies():
        copy.start()

    barrier = pltpu.get_barrier_semaphore()

    def greet(at):
        def one(i):
            _, device = at(i)
            pl.semaphore_signal(barrier, inc=1, device_id=device, device_id_type=MESH)

        return one

    loop(depth - 1, greet(at_depth))
    loop(planes - 1, greet(at_plane))
    pl.semaphore_wait(barrier, planes + depth - 2)

    def send_all(phase, j, source, target):
        count, at, own = (depth, at_depth, z) if phase in (0, 3) else (planes, at_plane, g)
        pltpu.make_async_copy(source(own), target(own), recv_sem.at[phase, j]).start()

        def one(i):
            peer, device = at(i)
            pltpu.make_async_remote_copy(
                src_ref=source(peer),
                dst_ref=target(own),
                send_sem=send_sem.at[phase, j],
                recv_sem=recv_sem.at[phase, j],
                device_id=device,
                device_id_type=MESH,
            ).start()

        loop(count - 1, one)

    def exchange(source, target, j):
        outer, arrays, inner = source.shape[1:4]

        def one(i):
            flat[...] = source[j, :, i].astype(F32).reshape(slots, turns)
            for k in range(inner):
                target[j, k, i] = flat[pl.ds(k, outer, stride=inner), :].astype(BF16)

        loop(arrays, one)

    def enter(j):
        for copy in load_copies(j):
            copy.wait()
        send_all(
            0,
            j,
            lambda peer: held.at[j, :, pl.ds(pl.multiple_of(peer * planes, planes), planes)],
            lambda own: own_in.at[j, own],
        )

    loop(chunks, enter)
    for copy in table_copies():
        copy.wait()

    row_of = lax.broadcasted_iota(jnp.int32, (slots, turns), 0)
    odd = lax.rem(row_of, 2) == 1
    edge_row = lax.broadcasted_iota(jnp.int32, (planes, turns), 0)
    edge_lane = lax.broadcasted_iota(jnp.int32, (planes, turns), 1)

    def earlier(now):
        edge = pltpu.roll(now[slots - planes :], 2, 0)
        wrapped = jnp.where(edge_lane == 0, 0.0, pltpu.roll(edge, 1, 1))
        edge = jnp.where(edge_row < 2, wrapped, edge)
        second = jnp.concatenate([edge, now[: slots - planes]], axis=0)
        return jnp.where(odd, pltpu.roll(now, 1, 0), pltpu.roll(second, slots - 1, 0)), second

    def later(now):
        edge = pltpu.roll(now[:planes], planes - 2, 0)
        wrapped = jnp.where(edge_lane == turns - 1, 0.0, pltpu.roll(edge, turns - 1, 1))
        edge = jnp.where(edge_row >= planes - 2, wrapped, edge)
        second = jnp.concatenate([now[planes:], edge], axis=0)
        return jnp.where(odd, pltpu.roll(second, 1, 0), pltpu.roll(now, slots - 1, 0)), second

    def transform():
        width = min(256, 2 * slots)

        def columns(i):
            at = pl.ds(pl.multiple_of(i * width, width), width)
            high, low = factors[0], factors[1]
            spectra[:, at] = dot(high, block[0, :, at]) + (
                dot(low, block[0, :, at]) + dot(high, block[1, :, at])
            )

        loop(2 * slots // width, columns)

    def put(i, real, imag):
        rows = pl.ds(i * PAD, PAD)
        for side, part in ((0, real), (slots, imag)):
            high, low = split(part)
            factors[0, rows, pl.ds(side, slots)] = high
            factors[1, rows, pl.ds(side, slots)] = low

    def get(i):
        rows = pl.ds(i * PAD, PAD)
        return spectra[rows, pl.ds(0, slots)], spectra[rows, pl.ds(slots, slots)]

    def own_channel(j):
        await_bytes(own_in.at[j], recv_sem.at[0, j])
        exchange(own_in, leaving_in, j)
        send_all(1, j, lambda peer: leaving_in.at[j, peer], lambda own: arrived_in.at[j, own])
        await_bytes(arrived_in.at[j], recv_sem.at[1, j])
        exchange(arrived_in, own_in, j)

        mine = pl.ds(pl.multiple_of(j * slots, slots), slots)
        here = lax.broadcasted_iota(jnp.int32, (1, slots), 1) == z * planes + g

        def pick(values):
            return jnp.sum(jnp.where(here, values, 0.0), axis=1, keepdims=True)

        tap = [[pick(taps[i, pl.ds(t, 1), mine]) for t in range(3)] for i in range(3)]
        gain = pick(gains[:, mine])

        def line(i):
            return own_in[j, :, i].astype(F32).reshape(slots, turns)

        def feature(i):
            now = line(i)
            first_back, second_back = earlier(now)
            return (
                tap[i][0] * now
                + tap[i][1] * first_back
                + tap[i][2] * second_back
            )

        lines[0] = feature(1)
        lines[1] = feature(2)
        lines[2] = lines[0] * lines[1]
        lines[3] = line(3)
        lines[4] = feature(0) * line(4)

        def spectrum(i):
            high, low = split(lines[2 + i])
            turned = dot_t(first[0], high) + (dot_t(first[0], low) + dot_t(first[1], high))
            real, imag = turned[:PAD], turned[PAD:]
            put(i, real * twist[0] + imag * twist[1], imag * twist[0] - real * twist[1])

        for i in range(3):
            spectrum(i)
        transform()
        gated_re, gated_im = get(0)
        filt_re, filt_im = get(1)
        put(
            0,
            gated_re * filt_re - gated_im * filt_im,
            -(gated_re * filt_im) - gated_im * filt_re,
        )
        gated_re, gated_im = get(0)
        filt_re, filt_im = get(1)
        side_re, side_im = get(2)
        put(
            1,
            side_re * filt_re + side_im * filt_im,
            side_re * filt_im - side_im * filt_re,
        )
        put(
            2,
            side_re * gated_re + side_im * gated_im,
            side_re * gated_im - side_im * gated_re,
        )
        transform()

        def back(i):
            real, imag = get(i)
            turned = jnp.concatenate(
                [real * twist[0] + imag * twist[1], imag * twist[0] - real * twist[1]], axis=0
            )
            high, low = split(turned)
            result = dot(last[0], high) + (dot(last[0], low) + dot(last[1], high))
            return jnp.transpose(result)

        lines[2] = back(0) + gain * lines[2]
        lines[4] = back(1) + gain * lines[4]
        own_out[j, :, 3] = back(2).astype(BF16).reshape(depth, planes, turns)

        def leave(i, grad):
            now = grad.astype(BF16).astype(F32)
            first_next, second_next = later(now)
            total = (
                tap[i][0] * now
                + tap[i][1] * first_next
                + tap[i][2] * second_next
            )
            own_out[j, :, i] = total.astype(BF16).reshape(depth, planes, turns)

        leave(0, line(4) * lines[2])
        leave(1, lines[4] * lines[1])
        leave(2, lines[4] * lines[0])
        exchange(own_out, leaving_out, j)
        send_all(2, j, lambda peer: leaving_out.at[j, peer], lambda own: arrived_out.at[j, own])
        await_bytes(arrived_out.at[j], recv_sem.at[2, j])
        exchange(arrived_out, own_out, j)
        send_all(
            3,
            j,
            lambda peer: own_out.at[j, peer],
            lambda own: returned.at[j, :, pl.ds(pl.multiple_of(own * planes, planes), planes)],
        )

    loop(chunks, own_channel)

    def finish(j):
        await_bytes(returned.at[j], recv_sem.at[3, j])
        for copy in out_copies(j):
            copy.start()

    loop(chunks, finish)

    def close(j):
        for copy in out_copies(j):
            copy.wait()
        await_bytes(held.at[j, :, pl.ds(0, (depth - 1) * planes)], send_sem.at[0, j])
        await_bytes(leaving_in.at[j, pl.ds(0, planes - 1)], send_sem.at[1, j])
        await_bytes(leaving_out.at[j, pl.ds(0, planes - 1)], send_sem.at[2, j])
        await_bytes(own_out.at[j, pl.ds(0, depth - 1)], send_sem.at[3, j])

    loop(chunks, close)


def hand_over(filter_in, projected_in, filter_out, projected_out):
    filter_out[...] = filter_in[...]
    projected_out[...] = projected_in[...]


def on_device(projected, short_taps, long_filter, skip_gain, cotangent):
    channels = short_taps.shape[1]
    turns = projected.shape[-1]
    rows = lax.axis_size("row")
    depth = lax.axis_size("col") // 2
    planes = rows * 2
    slots = planes * depth
    chunks = channels // slots
    made = [jnp.asarray(t) for t in tables(turns, planes, depth)]
    anywhere = pl.BlockSpec(memory_space=pl.ANY)

    def vmem(*shape, dtype=BF16):
        return pltpu.VMEM(shape, dtype)

    filter_grad, projected_grad = pl.pallas_call(
        functools.partial(kernel, planes, depth),
        out_shape=(
            jax.ShapeDtypeStruct((channels, turns), BF16),
            jax.ShapeDtypeStruct((3, channels, turns), BF16),
        ),
        in_specs=[anywhere] * 9,
        out_specs=(anywhere, anywhere),
        scratch_shapes=[
            vmem(chunks, 5, slots, turns),
            vmem(chunks, depth, 5, planes, turns),
            vmem(chunks, planes, 5, depth, turns),
            vmem(chunks, planes, 5, depth, turns),
            vmem(chunks, depth, 4, planes, turns),
            vmem(chunks, planes, 4, depth, turns),
            vmem(chunks, planes, 4, depth, turns),
            vmem(chunks, 4, slots, turns),
            vmem(3, 3, channels, dtype=F32),
            vmem(1, channels, dtype=F32),
            *[pltpu.VMEM(t.shape, t.dtype) for t in made],
            vmem(slots, turns, dtype=F32),
            vmem(5, slots, turns, dtype=F32),
            vmem(3 * PAD, 2 * slots, dtype=F32),
            vmem(2, 3 * PAD, 2 * slots),
            pltpu.SemaphoreType.DMA((chunks, 3)),
            pltpu.SemaphoreType.DMA((6,)),
            pltpu.SemaphoreType.DMA((4, chunks)),
            pltpu.SemaphoreType.DMA((4, chunks)),
            pltpu.SemaphoreType.DMA((chunks, 2)),
        ],
        compiler_params=pltpu.CompilerParams(
            collective_id=0, has_side_effects=True, vmem_limit_bytes=56 << 20
        ),
    )(
        jnp.swapaxes(short_taps, 1, 2),
        skip_gain.reshape(1, channels),
        projected.reshape(3, channels, turns),
        long_filter.reshape(channels, turns),
        cotangent.reshape(channels, turns),
        *made,
    )
    part = channels // 4
    blocks = (
        pl.BlockSpec((part, turns), lambda i: (i, 0)),
        pl.BlockSpec((3, part, turns), lambda i: (0, i, 0)),
    )
    filter_grad, projected_grad = pl.pallas_call(
        hand_over,
        out_shape=(
            jax.ShapeDtypeStruct((channels, turns), BF16),
            jax.ShapeDtypeStruct((3, channels, turns), BF16),
        ),
        grid=(4,),
        in_specs=blocks,
        out_specs=blocks,
        compiler_params=pltpu.CompilerParams(vmem_limit_bytes=56 << 20),
    )(filter_grad, projected_grad)
    return (
        filter_grad.reshape(channels, 1, 1, turns),
        projected_grad.reshape(3, channels, 1, 1, turns),
    )


def solution(mesh):
    in_specs = (
        P(None, None, "row", "col", None),
        P(),
        P(None, "row", "col", None),
        P(),
        P(None, "row", "col", None),
    )
    out_specs = (P(None, "row", "col", None), P(None, None, "row", "col", None))
    return jax.shard_map(
        on_device, mesh=mesh, in_specs=in_specs, out_specs=out_specs, check_vma=False
    )
```

```python
import functools
import math

import jax
import jax.numpy as jnp
import numpy as np
from jax import lax
from jax.experimental import pallas as pl
from jax.experimental.pallas import tpu as pltpu
from jax.sharding import PartitionSpec as P

MESH = pl.DeviceIdType.MESH
BF16 = jnp.bfloat16
F32 = jnp.float32
PAD = 80


def two(table):
    high = table.astype(np.float32).astype(BF16)
    low = (table - high.astype(np.float64)).astype(np.float32).astype(BF16)
    return np.stack([high, low])


def tables(turns, planes, depth):
    slots = planes * depth
    length = turns * slots
    half = turns // 2 + 1
    z, g = np.meshgrid(np.arange(depth), np.arange(planes), indexing="ij")
    r = ((g // 2) * 2 * depth + z * 2 + g % 2).reshape(-1)
    k = np.arange(half)
    angles = 2.0 * math.pi * (np.outer(k, np.arange(turns)) % turns) / turns
    weight = np.where((k == 0) | (k == turns // 2), 1.0, 2.0)[:, None]
    scale = 1.0 / length * length**-0.5

    def padded(table):
        return np.pad(table, [(0, PAD - half), (0, 0)])

    cosine, sine = padded(np.cos(angles)), padded(np.sin(angles))
    first = np.concatenate([cosine, -sine])
    weight = padded(weight) * scale
    last = np.concatenate([weight * cosine, weight * sine]).T
    angles = 2.0 * math.pi * np.outer(k, r) / length
    twist = np.stack([padded(np.cos(angles)), padded(np.sin(angles))]).astype(np.float32)
    angles = 2.0 * math.pi * (np.outer(r, r) % slots) / slots
    cosine, sine = np.cos(angles), np.sin(angles)
    block = np.block([[cosine, -sine], [sine, cosine]])
    return two(first), two(last), twist, two(block)


def split(values):
    high = values.astype(BF16)
    return high, (values - high.astype(F32)).astype(BF16)


def dot(left, right):
    return jnp.dot(left, right, preferred_element_type=F32)


def dot_t(left, right):
    return lax.dot_general(left, right, (((1,), (1,)), ((), ())), preferred_element_type=F32)


def kernel(
    planes,
    depth,
    taps_hbm,
    gains_hbm,
    projected,
    filt,
    cotangent,
    first_hbm,
    last_hbm,
    twist_hbm,
    block_hbm,
    filter_out,
    projected_out,
    raw,
    raw_near,
    filter_in,
    products,
    kept,
    own_in,
    leaving_in,
    arrived_in,
    own_out,
    leaving_out,
    arrived_out,
    returned,
    grads,
    grads_near,
    result,
    columns_of,
    taps,
    gains,
    first,
    last,
    twist,
    block,
    flat,
    spectra,
    factors,
    load_sem,
    table_sem,
    send_sem,
    recv_sem,
    halo_send,
    halo_recv,
    out_sem,
):
    chunks = filter_in.shape[0]
    turns = filter_in.shape[-1]
    slots = planes * depth
    half = slots // 2
    rows_all = planes // 2
    row = lax.axis_index("row")
    col = lax.axis_index("col")
    z = col // 2
    y = lax.rem(col, 2)
    g = row * 2 + y
    rank = row * 2 * depth + col

    def at_plane(step):
        peer = lax.rem(g + step + 1, planes)
        return peer, (peer // 2, z * 2 + lax.rem(peer, 2))

    def at_depth(step):
        away = (1 - 2 * lax.rem(step, 2)) * (step // 2 + 1)
        peer = lax.rem(z + away + depth, depth)
        return peer, (row, peer * 2 + y)

    up, down = z + 1, z + depth - 1
    two_later = (lax.rem(row + up // depth, rows_all), lax.rem(up, depth) * 2 + y)
    two_earlier = (
        lax.rem(row + rows_all - 1 + down // depth, rows_all),
        lax.rem(down, depth) * 2 + y,
    )
    partner = (row, z * 2 + 1 - y)
    sides = (pl.ds(0, half), pl.ds(half, half))

    def await_bytes(ref, sem):
        pltpu.make_async_copy(ref, ref, sem).wait()

    def load_copies(j):
        rows = pl.ds(j * slots, slots)
        return (
            pltpu.make_async_copy(
                projected.at[:, rows], raw.at[j, 0, pl.ds(0, 3)], load_sem.at[j, 0]
            ),
            pltpu.make_async_copy(cotangent.at[rows], raw.at[j, 0, 3], load_sem.at[j, 1]),
            pltpu.make_async_copy(filt.at[rows], filter_in.at[j], load_sem.at[j, 2]),
        )

    def table_copies():
        pairs = (
            (taps_hbm, taps),
            (gains_hbm, gains),
            (first_hbm, first),
            (last_hbm, last),
            (twist_hbm, twist),
            (block_hbm, block),
        )
        return [
            pltpu.make_async_copy(source, target, table_sem.at[i])
            for i, (source, target) in enumerate(pairs)
        ]

    def out_copies(j):
        rows = pl.ds(j * slots, slots)
        return (
            pltpu.make_async_copy(result.at[j], projected_out.at[:, rows], out_sem.at[j, 0]),
            pltpu.make_async_copy(returned.at[j, 2], filter_out.at[rows], out_sem.at[j, 1]),
        )

    def halo(kind, j, source, target, device):
        return pltpu.make_async_remote_copy(
            src_ref=source,
            dst_ref=target,
            send_sem=halo_send.at[kind, j],
            recv_sem=halo_recv.at[kind, j],
            device_id=device,
            device_id_type=MESH,
        )

    def far_halo(way, side, j):
        arrays = pl.ds(0, 4 if (way, side) == (0, 1) else 3)
        held = (raw, grads)[way]
        return halo(
            way * 2 + side,
            j,
            held.at[j, 0, arrays, sides[side]],
            held.at[j, 1, arrays, sides[side]],
            two_later if way == side else two_earlier,
        )

    def near_halo(way, side, j):
        held, near = ((raw, raw_near), (grads, grads_near))[way]
        own_or_far = y if way == side else 1 - y
        return halo(
            4 + way * 2 + side,
            j,
            held.at[j, own_or_far, pl.ds(0, 3), sides[side]],
            near.at[j, :, sides[side]],
            partner,
        )

    def loop(count, body):
        lax.fori_loop(0, count, lambda i, carry: (body(i), carry)[1], 0)

    for j in range(chunks):
        for copy in load_copies(j):
            copy.start()
    for copy in table_copies():
        copy.start()

    barrier = pltpu.get_barrier_semaphore()

    def greet(at):
        def one(i):
            _, device = at(i)
            pl.semaphore_signal(barrier, inc=1, device_id=device, device_id_type=MESH)

        return one

    loop(depth - 1, greet(at_depth))
    loop(planes - 1, greet(at_plane))
    for device in (two_later, two_earlier):
        pl.semaphore_signal(barrier, inc=1, device_id=device, device_id_type=MESH)
    pl.semaphore_wait(barrier, planes + depth)

    def send_all(phase, j, source, target):
        count, at, own = (planes, at_plane, g) if phase in (2, 3) else (depth, at_depth, z)
        pltpu.make_async_copy(source(own), target(own), recv_sem.at[phase, j]).start()

        def one(i):
            peer, device = at(i)
            pltpu.make_async_remote_copy(
                src_ref=source(peer),
                dst_ref=target(own),
                send_sem=send_sem.at[phase, j],
                recv_sem=recv_sem.at[phase, j],
                device_id=device,
                device_id_type=MESH,
            ).start()

        loop(count - 1, one)

    def exchange(source, target, j):
        outer, arrays, inner = source.shape[1:4]

        def one(i):
            flat[...] = source[j, :, i].astype(F32).reshape(slots, turns)
            for k in range(inner):
                target[j, k, i] = flat[pl.ds(k, outer, stride=inner), :].astype(BF16)

        loop(arrays, one)

    def part(peer):
        return pl.ds(pl.multiple_of(peer * planes, planes), planes)

    def enter(j):
        for copy in load_copies(j):
            copy.wait()
        for side in range(2):
            far_halo(0, side, j).start()
        send_all(0, j, lambda peer: filter_in.at[j, part(peer)], lambda own: own_in.at[j, own, 0])

    loop(chunks, enter)
    for copy in table_copies():
        copy.wait()

    def make_columns(j):
        mine = pl.ds(pl.multiple_of(j * slots, slots), slots)
        which = lax.broadcasted_iota(jnp.int32, (16, slots), 0)
        packed = jnp.where(which == 9, gains[:, mine], 0.0)
        for i in range(3):
            for t in range(3):
                packed = jnp.where(which == i * 3 + t, taps[i, pl.ds(t, 1), mine], packed)
        columns_of[j] = jnp.transpose(packed)

    loop(chunks, make_columns)

    lane = lax.broadcasted_iota(jnp.int32, (half, turns), 1)
    ranks = jnp.full((half, turns), rank, jnp.int32)
    final = lane == turns - 1
    last_two, last_one, next_last = ranks >= slots - 2, ranks == slots - 1, ranks == slots - 2
    first_two, first_one = ranks < 2, ranks == 0

    def wrap_back(values, where, fill):
        moved = pltpu.roll(values, 1, 1)
        if fill:
            moved = jnp.where(lane == 0, 0.0, moved)
        return jnp.where(where, moved, values)

    def wrap_ahead(values, where, fill):
        moved = pltpu.roll(values, turns - 1, 1)
        if fill:
            moved = jnp.where(final, 0.0, moved)
        return jnp.where(where, moved, values)

    def drop(values, where):
        return jnp.where(jnp.logical_and(final, where), 0.0, values)

    def column(j, side, k):
        return columns_of[j, sides[side], pl.ds(k, 1)]

    def filtered(j, side, i, lines):
        return (
            column(j, side, i * 3) * lines[0]
            + column(j, side, i * 3 + 1) * lines[1]
            + column(j, side, i * 3 + 2) * lines[2]
        )

    def pass_near(way):
        def one(j):
            for side in range(2):
                far_halo(way, side, j).wait_recv()
                near_halo(way, side, j).start()

        return one

    def make_products(j):
        for side in range(2):
            rows = sides[side]
            near_halo(0, side, j).wait_recv()

            def feature(i):
                own = raw[j, 0, i, rows].astype(F32)
                near = raw_near[j, i, rows].astype(F32)
                far = raw[j, 1, i, rows].astype(F32)
                if side == 0:
                    near = wrap_back(near, first_one, True)
                    far = wrap_back(far, first_two, True)
                    return filtered(j, side, i, (own, near, far))
                far = wrap_ahead(far, last_two, False)
                near = drop(wrap_ahead(near, last_one, False), next_last)
                return filtered(j, side, i, (far, near, drop(own, last_two)))

            if side == 0:
                seed = raw[j, 0, 3, rows].astype(F32)
            else:
                seed = wrap_ahead(raw[j, 1, 3, rows].astype(F32), last_two, False)
            kept[j, 3, rows] = seed
            weighted = feature(0) * seed
            kept[j, 2, rows] = weighted
            products[j, 1, rows] = weighted.astype(BF16)
            keys = feature(1)
            kept[j, 0, rows] = keys
            values = feature(2)
            kept[j, 1, rows] = values
            products[j, 0, rows] = (keys * values).astype(BF16)
        send_all(
            1,
            j,
            lambda peer: products.at[j, :, part(peer)],
            lambda own: own_in.at[j, own, pl.ds(1, 2)],
        )

    def products_in_turn(j):
        @pl.when(j + 1 < chunks)
        def _():
            pass_near(0)(j + 1)

        make_products(j)

    pass_near(0)(0)
    loop(chunks, products_in_turn)

    def transform():
        width = min(256, 2 * slots)

        def columns(i):
            at = pl.ds(pl.multiple_of(i * width, width), width)
            high, low = factors[0], factors[1]
            spectra[:, at] = dot(high, block[0, :, at]) + (
                dot(low, block[0, :, at]) + dot(high, block[1, :, at])
            )

        loop(2 * slots // width, columns)

    def put(i, real, imag):
        rows = pl.ds(i * PAD, PAD)
        for side, part in ((0, real), (slots, imag)):
            high, low = split(part)
            factors[0, rows, pl.ds(side, slots)] = high
            factors[1, rows, pl.ds(side, slots)] = low

    def get(i):
        rows = pl.ds(i * PAD, PAD)
        return spectra[rows, pl.ds(0, slots)], spectra[rows, pl.ds(slots, slots)]

    def own_channel(j):
        await_bytes(own_in.at[j, :, 0], recv_sem.at[0, j])
        await_bytes(own_in.at[j, :, pl.ds(1, 2)], recv_sem.at[1, j])
        exchange(own_in, leaving_in, j)
        send_all(2, j, lambda peer: leaving_in.at[j, peer], lambda own: arrived_in.at[j, own])
        await_bytes(arrived_in.at[j], recv_sem.at[2, j])
        exchange(arrived_in, own_in, j)

        def spectrum(i):
            line = own_in[j, :, i].reshape(slots, turns)
            turned = dot_t(first[0], line) + dot_t(first[1], line)
            real, imag = turned[:PAD], turned[PAD:]
            put(i, real * twist[0] + imag * twist[1], imag * twist[0] - real * twist[1])

        for i in range(3):
            spectrum(i)
        transform()
        filt_re, filt_im = get(0)
        gated_re, gated_im = get(1)
        put(
            0,
            gated_re * filt_re - gated_im * filt_im,
            -(gated_re * filt_im) - gated_im * filt_re,
        )
        side_re, side_im = get(2)
        put(
            1,
            side_re * filt_re + side_im * filt_im,
            side_re * filt_im - side_im * filt_re,
        )
        put(
            2,
            side_re * gated_re + side_im * gated_im,
            side_re * gated_im - side_im * gated_re,
        )
        transform()

        def back(i):
            real, imag = get(i)
            turned = jnp.concatenate(
                [real * twist[0] + imag * twist[1], imag * twist[0] - real * twist[1]], axis=0
            )
            high, low = split(turned)
            line = dot(last[0], high) + (dot(last[0], low) + dot(last[1], high))
            own_out[j, :, i] = jnp.transpose(line).astype(BF16).reshape(depth, planes, turns)

        for i in range(3):
            back(i)
        exchange(own_out, leaving_out, j)
        send_all(3, j, lambda peer: leaving_out.at[j, peer], lambda own: arrived_out.at[j, own])
        await_bytes(arrived_out.at[j], recv_sem.at[3, j])
        exchange(arrived_out, own_out, j)
        send_all(
            4, j, lambda peer: own_out.at[j, peer], lambda own: returned.at[j, :, part(own)]
        )

    loop(chunks, own_channel)

    def make_grads(j):
        await_bytes(returned.at[j], recv_sem.at[4, j])
        out_copies(j)[1].start()
        for side in range(2):
            rows = sides[side]
            gain = column(j, side, 9)
            keys, values = kept[j, 0, rows], kept[j, 1, rows]
            mixed = returned[j, 0, rows].astype(F32) + gain * (keys * values)
            grads[j, 0, 0, rows] = (kept[j, 3, rows] * mixed).astype(BF16)
            gated_grad = returned[j, 1, rows].astype(F32) + gain * kept[j, 2, rows]
            grads[j, 0, 1, rows] = (gated_grad * values).astype(BF16)
            grads[j, 0, 2, rows] = (gated_grad * keys).astype(BF16)
            far_halo(1, side, j).start()

    loop(chunks, make_grads)
    loop(chunks, pass_near(1))

    def finish(j):
        for side in range(2):
            rows = sides[side]
            near_halo(1, side, j).wait_recv()
            for i in range(3):
                own = grads[j, 0, i, rows].astype(F32)
                near = grads_near[j, i, rows].astype(F32)
                far = grads[j, 1, i, rows].astype(F32)
                if side == 0:
                    near = wrap_ahead(near, last_one, True)
                    far = wrap_ahead(far, last_two, True)
                    total = filtered(j, side, i, (own, near, far))
                else:
                    far = wrap_back(far, first_two, False)
                    near = drop(wrap_back(near, first_one, False), last_one)
                    total = filtered(j, side, i, (far, near, drop(own, last_two)))
                result[j, i, rows] = total.astype(BF16)
        out_copies(j)[0].start()

    loop(chunks, finish)

    def close(j):
        for copy in out_copies(j):
            copy.wait()
        others = pl.ds(0, (depth - 1) * planes)
        await_bytes(filter_in.at[j, others], send_sem.at[0, j])
        await_bytes(products.at[j, :, others], send_sem.at[1, j])
        await_bytes(leaving_in.at[j, pl.ds(0, planes - 1)], send_sem.at[2, j])
        await_bytes(leaving_out.at[j, pl.ds(0, planes - 1)], send_sem.at[3, j])
        await_bytes(own_out.at[j, pl.ds(0, depth - 1)], send_sem.at[4, j])
        for way in range(2):
            for side in range(2):
                far_halo(way, side, j).wait_send()
                near_halo(way, side, j).wait_send()

    loop(chunks, close)


def hand_over(filter_in, projected_in, filter_out, projected_out):
    filter_out[...] = filter_in[...]
    projected_out[...] = projected_in[...]


def on_device(projected, short_taps, long_filter, skip_gain, cotangent):
    channels = short_taps.shape[1]
    turns = projected.shape[-1]
    rows = lax.axis_size("row")
    depth = lax.axis_size("col") // 2
    planes = rows * 2
    slots = planes * depth
    chunks = channels // slots
    made = [jnp.asarray(t) for t in tables(turns, planes, depth)]
    anywhere = pl.BlockSpec(memory_space=pl.ANY)

    def vmem(*shape, dtype=BF16):
        return pltpu.VMEM(shape, dtype)

    filter_grad, projected_grad = pl.pallas_call(
        functools.partial(kernel, planes, depth),
        out_shape=(
            jax.ShapeDtypeStruct((channels, turns), BF16),
            jax.ShapeDtypeStruct((3, channels, turns), BF16),
        ),
        in_specs=[anywhere] * 9,
        out_specs=(anywhere, anywhere),
        scratch_shapes=[
            vmem(chunks, 2, 4, slots, turns),
            vmem(chunks, 3, slots, turns),
            vmem(chunks, slots, turns),
            vmem(chunks, 2, slots, turns),
            vmem(chunks, 4, slots, turns, dtype=F32),
            vmem(chunks, depth, 3, planes, turns),
            vmem(chunks, planes, 3, depth, turns),
            vmem(chunks, planes, 3, depth, turns),
            vmem(chunks, depth, 3, planes, turns),
            vmem(chunks, planes, 3, depth, turns),
            vmem(chunks, planes, 3, depth, turns),
            vmem(chunks, 3, slots, turns),
            vmem(chunks, 2, 3, slots, turns),
            vmem(chunks, 3, slots, turns),
            vmem(chunks, 3, slots, turns),
            vmem(chunks, slots, 16, dtype=F32),
            vmem(3, 3, channels, dtype=F32),
            vmem(1, channels, dtype=F32),
            *[pltpu.VMEM(t.shape, t.dtype) for t in made],
            vmem(slots, turns, dtype=F32),
            vmem(3 * PAD, 2 * slots, dtype=F32),
            vmem(2, 3 * PAD, 2 * slots),
            pltpu.SemaphoreType.DMA((chunks, 3)),
            pltpu.SemaphoreType.DMA((6,)),
            pltpu.SemaphoreType.DMA((5, chunks)),
            pltpu.SemaphoreType.DMA((5, chunks)),
            pltpu.SemaphoreType.DMA((8, chunks)),
            pltpu.SemaphoreType.DMA((8, chunks)),
            pltpu.SemaphoreType.DMA((chunks, 2)),
        ],
        compiler_params=pltpu.CompilerParams(
            collective_id=0, has_side_effects=True, vmem_limit_bytes=56 << 20
        ),
    )(
        jnp.swapaxes(short_taps, 1, 2),
        skip_gain.reshape(1, channels),
        projected.reshape(3, channels, turns),
        long_filter.reshape(channels, turns),
        cotangent.reshape(channels, turns),
        *made,
    )
    part = channels // 4
    blocks = (
        pl.BlockSpec((part, turns), lambda i: (i, 0)),
        pl.BlockSpec((3, part, turns), lambda i: (0, i, 0)),
    )
    filter_grad, projected_grad = pl.pallas_call(
        hand_over,
        out_shape=(
            jax.ShapeDtypeStruct((channels, turns), BF16),
            jax.ShapeDtypeStruct((3, channels, turns), BF16),
        ),
        grid=(4,),
        in_specs=blocks,
        out_specs=blocks,
        compiler_params=pltpu.CompilerParams(vmem_limit_bytes=56 << 20),
    )(filter_grad, projected_grad)
    return (
        filter_grad.reshape(channels, 1, 1, turns),
        projected_grad.reshape(3, channels, 1, 1, turns),
    )


def solution(mesh):
    in_specs = (
        P(None, None, "row", "col", None),
        P(),
        P(None, "row", "col", None),
        P(),
        P(None, "row", "col", None),
    )
    out_specs = (P(None, "row", "col", None), P(None, None, "row", "col", None))
    return jax.shard_map(
        on_device, mesh=mesh, in_specs=in_specs, out_specs=out_specs, check_vma=False
    )
```

```python
import functools
import math

import jax
import jax.numpy as jnp
import numpy as np
from jax import lax
from jax.experimental import pallas as pl
from jax.experimental.pallas import tpu as pltpu
from jax.sharding import PartitionSpec as P

MESH = pl.DeviceIdType.MESH
BF16 = jnp.bfloat16
F32 = jnp.float32
PAD = 80


def two(table):
    high = table.astype(np.float32).astype(BF16)
    low = (table - high.astype(np.float64)).astype(np.float32).astype(BF16)
    return np.stack([high, low])


def tables(turns, planes, depth):
    slots = planes * depth
    length = turns * slots
    half = turns // 2 + 1
    z, g = np.meshgrid(np.arange(depth), np.arange(planes), indexing="ij")
    r = ((g // 2) * 2 * depth + z * 2 + g % 2).reshape(-1)
    k = np.arange(half)
    angles = 2.0 * math.pi * (np.outer(k, np.arange(turns)) % turns) / turns
    weight = np.where((k == 0) | (k == turns // 2), 1.0, 2.0)[:, None]
    scale = 1.0 / length * length**-0.5

    def padded(table):
        return np.pad(table, [(0, PAD - half), (0, 0)])

    cosine, sine = padded(np.cos(angles)), padded(np.sin(angles))
    first = np.concatenate([cosine, -sine])
    weight = padded(weight) * scale
    last = np.concatenate([weight * cosine, weight * sine]).T
    angles = 2.0 * math.pi * np.outer(k, r) / length
    twist = np.stack([padded(np.cos(angles)), padded(np.sin(angles))]).astype(np.float32)
    angles = 2.0 * math.pi * (np.outer(r, r) % slots) / slots
    cosine, sine = np.cos(angles), np.sin(angles)
    block = np.block([[cosine, -sine], [sine, cosine]])
    return two(first), two(last), twist, two(block)


def split(values):
    high = values.astype(BF16)
    return high, (values - high.astype(F32)).astype(BF16)


def dot(left, right):
    return jnp.dot(left, right, preferred_element_type=F32)


def dot_t(left, right):
    return lax.dot_general(left, right, (((1,), (1,)), ((), ())), preferred_element_type=F32)


def kernel(
    planes,
    depth,
    taps_hbm,
    gains_hbm,
    projected,
    filt,
    cotangent,
    first_hbm,
    last_hbm,
    twist_hbm,
    block_hbm,
    filter_out,
    projected_out,
    raw,
    raw_near,
    filter_in,
    products,
    kept,
    own_in,
    leaving_in,
    arrived_in,
    own_out,
    leaving_out,
    arrived_out,
    returned,
    grads,
    grads_near,
    result,
    columns_of,
    whole_held,
    whole_in,
    whole_leaving_in,
    whole_arrived_in,
    whole_out,
    whole_leaving_out,
    whole_arrived_out,
    whole_returned,
    lines,
    taps,
    gains,
    first,
    last,
    twist,
    block,
    flat,
    spectra,
    factors,
    load_sem,
    table_sem,
    send_sem,
    recv_sem,
    halo_send,
    halo_recv,
    out_sem,
):
    chunks = filter_in.shape[0]
    turns = filter_in.shape[-1]
    slots = planes * depth
    half = slots // 2
    rows_all = planes // 2
    row = lax.axis_index("row")
    col = lax.axis_index("col")
    z = col // 2
    y = lax.rem(col, 2)
    g = row * 2 + y
    rank = row * 2 * depth + col

    def at_plane(step):
        peer = lax.rem(g + step + 1, planes)
        return peer, (peer // 2, z * 2 + lax.rem(peer, 2))

    def at_depth(step):
        away = (1 - 2 * lax.rem(step, 2)) * (step // 2 + 1)
        peer = lax.rem(z + away + depth, depth)
        return peer, (row, peer * 2 + y)

    up, down = z + 1, z + depth - 1
    two_later = (lax.rem(row + up // depth, rows_all), lax.rem(up, depth) * 2 + y)
    two_earlier = (
        lax.rem(row + rows_all - 1 + down // depth, rows_all),
        lax.rem(down, depth) * 2 + y,
    )
    partner = (row, z * 2 + 1 - y)
    sides = (pl.ds(0, half), pl.ds(half, half))

    def await_bytes(ref, sem):
        pltpu.make_async_copy(ref, ref, sem).wait()

    early, middle = depth // 2, depth * 5 // 8
    whole = chunks * slots

    def load_whole():
        rows = pl.ds(whole, slots)
        return (
            pltpu.make_async_copy(
                projected.at[:, rows], whole_held.at[0, pl.ds(0, 3)], load_sem.at[chunks, 0]
            ),
            pltpu.make_async_copy(filt.at[rows], whole_held.at[0, 3], load_sem.at[chunks, 1]),
            pltpu.make_async_copy(
                cotangent.at[rows], whole_held.at[0, 4], load_sem.at[chunks, 2]
            ),
        )

    def whole_copies():
        rows = pl.ds(whole, slots)
        return (
            pltpu.make_async_copy(
                whole_returned.at[0, pl.ds(0, 3)],
                projected_out.at[:, rows],
                out_sem.at[chunks, 0],
            ),
            pltpu.make_async_copy(
                whole_returned.at[0, 3], filter_out.at[rows], out_sem.at[chunks, 1]
            ),
        )

    def load_copies(j):
        rows = pl.ds(j * slots, slots)
        return (
            pltpu.make_async_copy(
                projected.at[:, rows], raw.at[j, 0, pl.ds(0, 3)], load_sem.at[j, 0]
            ),
            pltpu.make_async_copy(cotangent.at[rows], raw.at[j, 0, 3], load_sem.at[j, 1]),
            pltpu.make_async_copy(filt.at[rows], filter_in.at[j], load_sem.at[j, 2]),
        )

    def table_copies():
        pairs = (
            (taps_hbm, taps),
            (gains_hbm, gains),
            (first_hbm, first),
            (last_hbm, last),
            (twist_hbm, twist),
            (block_hbm, block),
        )
        return [
            pltpu.make_async_copy(source, target, table_sem.at[i])
            for i, (source, target) in enumerate(pairs)
        ]

    def out_copies(j):
        rows = pl.ds(j * slots, slots)
        return (
            pltpu.make_async_copy(result.at[j], projected_out.at[:, rows], out_sem.at[j, 0]),
            pltpu.make_async_copy(returned.at[j, 2], filter_out.at[rows], out_sem.at[j, 1]),
        )

    def halo(kind, j, source, target, device):
        return pltpu.make_async_remote_copy(
            src_ref=source,
            dst_ref=target,
            send_sem=halo_send.at[kind, j],
            recv_sem=halo_recv.at[kind, j],
            device_id=device,
            device_id_type=MESH,
        )

    def far_halo(way, side, j):
        arrays = pl.ds(0, 4 if (way, side) == (0, 1) else 3)
        held = (raw, grads)[way]
        return halo(
            way * 2 + side,
            j,
            held.at[j, 0, arrays, sides[side]],
            held.at[j, 1, arrays, sides[side]],
            two_later if way == side else two_earlier,
        )

    def near_halo(way, side, j):
        held, near = ((raw, raw_near), (grads, grads_near))[way]
        own_or_far = y if way == side else 1 - y
        return halo(
            4 + way * 2 + side,
            j,
            held.at[j, own_or_far, pl.ds(0, 3), sides[side]],
            near.at[j, :, sides[side]],
            partner,
        )

    def loop(count, body):
        lax.fori_loop(0, count, lambda i, carry: (body(i), carry)[1], 0)

    for j in range(chunks):
        for copy in load_copies(j):
            copy.start()
    for copy in load_whole():
        copy.start()
    for copy in table_copies():
        copy.start()

    barrier = pltpu.get_barrier_semaphore()

    def greet(at):
        def one(i):
            _, device = at(i)
            pl.semaphore_signal(barrier, inc=1, device_id=device, device_id_type=MESH)

        return one

    loop(depth - 1, greet(at_depth))
    loop(planes - 1, greet(at_plane))
    for device in (two_later, two_earlier):
        pl.semaphore_signal(barrier, inc=1, device_id=device, device_id_type=MESH)
    pl.semaphore_wait(barrier, planes + depth)

    def send_all(phase, j, source, target, start=0, stop=None):
        count, at, own = (planes, at_plane, g) if phase in (2, 3, 6, 7) else (depth, at_depth, z)
        stop = count - 1 if stop is None else stop
        if start == 0:
            pltpu.make_async_copy(source(own), target(own), recv_sem.at[phase, j]).start()

        def one(i):
            peer, device = at(i)
            pltpu.make_async_remote_copy(
                src_ref=source(peer),
                dst_ref=target(own),
                send_sem=send_sem.at[phase, j],
                recv_sem=recv_sem.at[phase, j],
                device_id=device,
                device_id_type=MESH,
            ).start()

        lax.fori_loop(start, stop, lambda i, carry: (one(i), carry)[1], 0)

    def exchange(source, target, j):
        outer, arrays, inner = source.shape[1:4]

        def one(i):
            flat[...] = source[j, :, i].astype(F32).reshape(slots, turns)
            for k in range(inner):
                target[j, k, i] = flat[pl.ds(k, outer, stride=inner), :].astype(BF16)

        loop(arrays, one)

    def part(peer):
        return pl.ds(pl.multiple_of(peer * planes, planes), planes)

    def enter(j):
        for copy in load_copies(j):
            copy.wait()
        for side in range(2):
            far_halo(0, side, j).start()
        send_all(0, j, lambda peer: filter_in.at[j, part(peer)], lambda own: own_in.at[j, own, 0])

    loop(chunks, enter)
    for copy in load_whole():
        copy.wait()
    for copy in table_copies():
        copy.wait()

    def make_columns(j):
        mine = pl.ds(pl.multiple_of(j * slots, slots), slots)
        which = lax.broadcasted_iota(jnp.int32, (16, slots), 0)
        packed = jnp.where(which == 9, gains[:, mine], 0.0)
        for i in range(3):
            for t in range(3):
                packed = jnp.where(which == i * 3 + t, taps[i, pl.ds(t, 1), mine], packed)
        columns_of[j] = jnp.transpose(packed)

    loop(chunks, make_columns)

    lane = lax.broadcasted_iota(jnp.int32, (half, turns), 1)
    ranks = jnp.full((half, turns), rank, jnp.int32)
    final = lane == turns - 1
    last_two, last_one, next_last = ranks >= slots - 2, ranks == slots - 1, ranks == slots - 2
    first_two, first_one = ranks < 2, ranks == 0

    def wrap_back(values, where, fill):
        moved = pltpu.roll(values, 1, 1)
        if fill:
            moved = jnp.where(lane == 0, 0.0, moved)
        return jnp.where(where, moved, values)

    def wrap_ahead(values, where, fill):
        moved = pltpu.roll(values, turns - 1, 1)
        if fill:
            moved = jnp.where(final, 0.0, moved)
        return jnp.where(where, moved, values)

    def drop(values, where):
        return jnp.where(jnp.logical_and(final, where), 0.0, values)

    def column(j, side, k):
        return columns_of[j, sides[side], pl.ds(k, 1)]

    def filtered(j, side, i, lines):
        return (
            column(j, side, i * 3) * lines[0]
            + column(j, side, i * 3 + 1) * lines[1]
            + column(j, side, i * 3 + 2) * lines[2]
        )

    def pass_near(way):
        def one(j):
            for side in range(2):
                far_halo(way, side, j).wait_recv()
                near_halo(way, side, j).start()

        return one

    def make_products(j):
        for side in range(2):
            rows = sides[side]
            near_halo(0, side, j).wait_recv()

            def feature(i):
                own = raw[j, 0, i, rows].astype(F32)
                near = raw_near[j, i, rows].astype(F32)
                far = raw[j, 1, i, rows].astype(F32)
                if side == 0:
                    near = wrap_back(near, first_one, True)
                    far = wrap_back(far, first_two, True)
                    return filtered(j, side, i, (own, near, far))
                far = wrap_ahead(far, last_two, False)
                near = drop(wrap_ahead(near, last_one, False), next_last)
                return filtered(j, side, i, (far, near, drop(own, last_two)))

            if side == 0:
                seed = raw[j, 0, 3, rows].astype(F32)
            else:
                seed = wrap_ahead(raw[j, 1, 3, rows].astype(F32), last_two, False)
            kept[j, 3, rows] = seed
            weighted = feature(0) * seed
            kept[j, 2, rows] = weighted
            products[j, 1, rows] = weighted.astype(BF16)
            keys = feature(1)
            kept[j, 0, rows] = keys
            values = feature(2)
            kept[j, 1, rows] = values
            products[j, 0, rows] = (keys * values).astype(BF16)
        send_all(
            1,
            j,
            lambda peer: products.at[j, :, part(peer)],
            lambda own: own_in.at[j, own, pl.ds(1, 2)],
        )

    def products_in_turn(j):
        @pl.when(j + 1 < chunks)
        def _():
            pass_near(0)(j + 1)

        make_products(j)

    pass_near(0)(0)
    loop(chunks, products_in_turn)
    send_all(
        5,
        0,
        lambda peer: whole_held.at[0, :, part(peer)],
        lambda own: whole_in.at[0, own],
    )

    def transform():
        width = min(256, 2 * slots)

        def columns(i):
            at = pl.ds(pl.multiple_of(i * width, width), width)
            high, low = factors[0], factors[1]
            spectra[:, at] = dot(high, block[0, :, at]) + (
                dot(low, block[0, :, at]) + dot(high, block[1, :, at])
            )

        loop(2 * slots // width, columns)

    def put(i, real, imag):
        rows = pl.ds(i * PAD, PAD)
        for side, part in ((0, real), (slots, imag)):
            high, low = split(part)
            factors[0, rows, pl.ds(side, slots)] = high
            factors[1, rows, pl.ds(side, slots)] = low

    def get(i):
        rows = pl.ds(i * PAD, PAD)
        return spectra[rows, pl.ds(0, slots)], spectra[rows, pl.ds(slots, slots)]

    row_of = lax.broadcasted_iota(jnp.int32, (slots, turns), 0)
    odd = lax.rem(row_of, 2) == 1
    edge_row = lax.broadcasted_iota(jnp.int32, (planes, turns), 0)
    edge_lane = lax.broadcasted_iota(jnp.int32, (planes, turns), 1)

    def earlier(now):
        edge = pltpu.roll(now[slots - planes :], 2, 0)
        wrapped = jnp.where(edge_lane == 0, 0.0, pltpu.roll(edge, 1, 1))
        edge = jnp.where(edge_row < 2, wrapped, edge)
        second = jnp.concatenate([edge, now[: slots - planes]], axis=0)
        return jnp.where(odd, pltpu.roll(now, 1, 0), pltpu.roll(second, slots - 1, 0)), second

    def later(now):
        edge = pltpu.roll(now[:planes], planes - 2, 0)
        wrapped = jnp.where(edge_lane == turns - 1, 0.0, pltpu.roll(edge, turns - 1, 1))
        edge = jnp.where(edge_row >= planes - 2, wrapped, edge)
        second = jnp.concatenate([now[planes:], edge], axis=0)
        return jnp.where(odd, pltpu.roll(second, 1, 0), pltpu.roll(now, slots - 1, 0)), second

    def spectral(analyse, keep):
        for i in range(3):
            turned = analyse(i)
            real, imag = turned[:PAD], turned[PAD:]
            put(i, real * twist[0] + imag * twist[1], imag * twist[0] - real * twist[1])
        transform()
        filt_re, filt_im = get(0)
        gated_re, gated_im = get(1)
        put(
            0,
            gated_re * filt_re - gated_im * filt_im,
            -(gated_re * filt_im) - gated_im * filt_re,
        )
        side_re, side_im = get(2)
        put(
            1,
            side_re * filt_re + side_im * filt_im,
            side_re * filt_im - side_im * filt_re,
        )
        put(
            2,
            side_re * gated_re + side_im * gated_im,
            side_re * gated_im - side_im * gated_re,
        )
        transform()

        for i in range(3):
            real, imag = get(i)
            turned = jnp.concatenate(
                [real * twist[0] + imag * twist[1], imag * twist[0] - real * twist[1]], axis=0
            )
            high, low = split(turned)
            line = dot(last[0], high) + (dot(last[0], low) + dot(last[1], high))
            keep(i, jnp.transpose(line))

    def whole_gather():
        await_bytes(whole_in.at[0], recv_sem.at[5, 0])
        exchange(whole_in, whole_leaving_in, 0)
        send_all(
            6,
            0,
            lambda peer: whole_leaving_in.at[0, peer],
            lambda own: whole_arrived_in.at[0, own],
        )

    def whole_channel():
        await_bytes(whole_arrived_in.at[0], recv_sem.at[6, 0])
        exchange(whole_arrived_in, whole_in, 0)
        mine = pl.ds(whole, slots)
        here = lax.broadcasted_iota(jnp.int32, (1, slots), 1) == z * planes + g

        def pick(values):
            return jnp.sum(jnp.where(here, values, 0.0), axis=1, keepdims=True)

        tap = [[pick(taps[i, pl.ds(t, 1), mine]) for t in range(3)] for i in range(3)]
        gain = pick(gains[:, mine])

        def line(i):
            return whole_in[0, :, i].astype(F32).reshape(slots, turns)

        def feature(i):
            now = line(i)
            first_back, second_back = earlier(now)
            return tap[i][0] * now + tap[i][1] * first_back + tap[i][2] * second_back

        lines[0] = line(3)
        lines[3] = feature(1)
        lines[4] = feature(2)
        lines[1] = lines[3] * lines[4]
        lines[2] = feature(0) * line(4)

        def analyse(i):
            high, low = split(lines[i])
            return dot_t(first[0], high) + (dot_t(first[0], low) + dot_t(first[1], high))

        def keep(i, result_line):
            if i == 2:
                whole_out[0, :, 3] = result_line.astype(BF16).reshape(depth, planes, turns)
            else:
                lines[1 + i] = result_line + gain * lines[1 + i]

        spectral(analyse, keep)

        def leave(i, grad):
            now = grad.astype(BF16).astype(F32)
            first_next, second_next = later(now)
            total = tap[i][0] * now + tap[i][1] * first_next + tap[i][2] * second_next
            whole_out[0, :, i] = total.astype(BF16).reshape(depth, planes, turns)

        leave(0, line(4) * lines[1])
        leave(1, lines[2] * lines[4])
        leave(2, lines[2] * lines[3])
        exchange(whole_out, whole_leaving_out, 0)
        send_all(
            7,
            0,
            lambda peer: whole_leaving_out.at[0, peer],
            lambda own: whole_arrived_out.at[0, own],
        )

    def whole_scatter():
        await_bytes(whole_arrived_out.at[0], recv_sem.at[7, 0])
        exchange(whole_arrived_out, whole_out, 0)

    def whole_back(start, stop):
        send_all(
            8,
            0,
            lambda peer: whole_out.at[0, peer],
            lambda own: whole_returned.at[0, :, part(own)],
            start,
            stop,
        )

    def gather(j):
        await_bytes(own_in.at[j, :, 0], recv_sem.at[0, j])
        await_bytes(own_in.at[j, :, pl.ds(1, 2)], recv_sem.at[1, j])
        exchange(own_in, leaving_in, j)
        send_all(2, j, lambda peer: leaving_in.at[j, peer], lambda own: arrived_in.at[j, own])

    def own_channel(j):
        await_bytes(arrived_in.at[j], recv_sem.at[2, j])
        exchange(arrived_in, own_in, j)

        def analyse(i):
            line = own_in[j, :, i].reshape(slots, turns)
            return dot_t(first[0], line) + dot_t(first[1], line)

        def keep(i, line):
            own_out[j, :, i] = line.astype(BF16).reshape(depth, planes, turns)

        spectral(analyse, keep)
        exchange(own_out, leaving_out, j)
        send_all(3, j, lambda peer: leaving_out.at[j, peer], lambda own: arrived_out.at[j, own])

    def scatter(j):
        await_bytes(arrived_out.at[j], recv_sem.at[3, j])
        exchange(arrived_out, own_out, j)
        send_all(
            4, j, lambda peer: own_out.at[j, peer], lambda own: returned.at[j, :, part(own)]
        )

    def channel_in_turn(j):
        own_channel(j)

        @pl.when(j + 1 < chunks)
        def _():
            gather(j + 1)

        @pl.when(j + 1 == chunks)
        def _():
            whole_gather()

        scatter(j)

    gather(0)
    loop(chunks, channel_in_turn)
    whole_channel()
    whole_scatter()
    whole_back(0, early)

    def make_grads(j):
        await_bytes(returned.at[j], recv_sem.at[4, j])
        out_copies(j)[1].start()
        for side in range(2):
            rows = sides[side]
            gain = column(j, side, 9)
            keys, values = kept[j, 0, rows], kept[j, 1, rows]
            mixed = returned[j, 0, rows].astype(F32) + gain * (keys * values)
            grads[j, 0, 0, rows] = (kept[j, 3, rows] * mixed).astype(BF16)
            gated_grad = returned[j, 1, rows].astype(F32) + gain * kept[j, 2, rows]
            grads[j, 0, 1, rows] = (gated_grad * values).astype(BF16)
            grads[j, 0, 2, rows] = (gated_grad * keys).astype(BF16)
            far_halo(1, side, j).start()

    loop(chunks - 1, make_grads)
    whole_back(early, middle)
    make_grads(chunks - 1)
    whole_back(middle, depth - 1)
    loop(chunks, pass_near(1))

    def finish(j):
        for side in range(2):
            rows = sides[side]
            near_halo(1, side, j).wait_recv()
            for i in range(3):
                own = grads[j, 0, i, rows].astype(F32)
                near = grads_near[j, i, rows].astype(F32)
                far = grads[j, 1, i, rows].astype(F32)
                if side == 0:
                    near = wrap_ahead(near, last_one, True)
                    far = wrap_ahead(far, last_two, True)
                    total = filtered(j, side, i, (own, near, far))
                else:
                    far = wrap_back(far, first_two, False)
                    near = drop(wrap_back(near, first_one, False), last_one)
                    total = filtered(j, side, i, (far, near, drop(own, last_two)))
                result[j, i, rows] = total.astype(BF16)
        out_copies(j)[0].start()

    loop(chunks, finish)
    await_bytes(whole_returned.at[0], recv_sem.at[8, 0])
    for copy in whole_copies():
        copy.start()

    def close(j):
        for copy in out_copies(j):
            copy.wait()
        others = pl.ds(0, (depth - 1) * planes)
        await_bytes(filter_in.at[j, others], send_sem.at[0, j])
        await_bytes(products.at[j, :, others], send_sem.at[1, j])
        await_bytes(leaving_in.at[j, pl.ds(0, planes - 1)], send_sem.at[2, j])
        await_bytes(leaving_out.at[j, pl.ds(0, planes - 1)], send_sem.at[3, j])
        await_bytes(own_out.at[j, pl.ds(0, depth - 1)], send_sem.at[4, j])
        for way in range(2):
            for side in range(2):
                far_halo(way, side, j).wait_send()
                near_halo(way, side, j).wait_send()

    loop(chunks, close)
    for copy in whole_copies():
        copy.wait()
    await_bytes(whole_held.at[0, :, pl.ds(0, (depth - 1) * planes)], send_sem.at[5, 0])
    await_bytes(whole_leaving_in.at[0, pl.ds(0, planes - 1)], send_sem.at[6, 0])
    await_bytes(whole_leaving_out.at[0, pl.ds(0, planes - 1)], send_sem.at[7, 0])
    await_bytes(whole_out.at[0, pl.ds(0, depth - 1)], send_sem.at[8, 0])


def hand_over(filter_in, projected_in, filter_out, projected_out):
    filter_out[...] = filter_in[...]
    projected_out[...] = projected_in[...]


def on_device(projected, short_taps, long_filter, skip_gain, cotangent):
    channels = short_taps.shape[1]
    turns = projected.shape[-1]
    rows = lax.axis_size("row")
    depth = lax.axis_size("col") // 2
    planes = rows * 2
    slots = planes * depth
    chunks = channels // slots - 1
    made = [jnp.asarray(t) for t in tables(turns, planes, depth)]
    anywhere = pl.BlockSpec(memory_space=pl.ANY)

    def vmem(*shape, dtype=BF16):
        return pltpu.VMEM(shape, dtype)

    filter_grad, projected_grad = pl.pallas_call(
        functools.partial(kernel, planes, depth),
        out_shape=(
            jax.ShapeDtypeStruct((channels, turns), BF16),
            jax.ShapeDtypeStruct((3, channels, turns), BF16),
        ),
        in_specs=[anywhere] * 9,
        out_specs=(anywhere, anywhere),
        scratch_shapes=[
            vmem(chunks, 2, 4, slots, turns),
            vmem(chunks, 3, slots, turns),
            vmem(chunks, slots, turns),
            vmem(chunks, 2, slots, turns),
            vmem(chunks, 4, slots, turns, dtype=F32),
            vmem(chunks, depth, 3, planes, turns),
            vmem(chunks, planes, 3, depth, turns),
            vmem(chunks, planes, 3, depth, turns),
            vmem(chunks, depth, 3, planes, turns),
            vmem(chunks, planes, 3, depth, turns),
            vmem(chunks, planes, 3, depth, turns),
            vmem(chunks, 3, slots, turns),
            vmem(chunks, 2, 3, slots, turns),
            vmem(chunks, 3, slots, turns),
            vmem(chunks, 3, slots, turns),
            vmem(chunks, slots, 16, dtype=F32),
            vmem(1, 5, slots, turns),
            vmem(1, depth, 5, planes, turns),
            vmem(1, planes, 5, depth, turns),
            vmem(1, planes, 5, depth, turns),
            vmem(1, depth, 4, planes, turns),
            vmem(1, planes, 4, depth, turns),
            vmem(1, planes, 4, depth, turns),
            vmem(1, 4, slots, turns),
            vmem(5, slots, turns, dtype=F32),
            vmem(3, 3, channels, dtype=F32),
            vmem(1, channels, dtype=F32),
            *[pltpu.VMEM(t.shape, t.dtype) for t in made],
            vmem(slots, turns, dtype=F32),
            vmem(3 * PAD, 2 * slots, dtype=F32),
            vmem(2, 3 * PAD, 2 * slots),
            pltpu.SemaphoreType.DMA((chunks + 1, 3)),
            pltpu.SemaphoreType.DMA((6,)),
            pltpu.SemaphoreType.DMA((9, chunks)),
            pltpu.SemaphoreType.DMA((9, chunks)),
            pltpu.SemaphoreType.DMA((8, chunks)),
            pltpu.SemaphoreType.DMA((8, chunks)),
            pltpu.SemaphoreType.DMA((chunks + 1, 2)),
        ],
        compiler_params=pltpu.CompilerParams(
            collective_id=0, has_side_effects=True, vmem_limit_bytes=56 << 20
        ),
    )(
        jnp.swapaxes(short_taps, 1, 2),
        skip_gain.reshape(1, channels),
        projected.reshape(3, channels, turns),
        long_filter.reshape(channels, turns),
        cotangent.reshape(channels, turns),
        *made,
    )
    part = channels // 4
    blocks = (
        pl.BlockSpec((part, turns), lambda i: (i, 0)),
        pl.BlockSpec((3, part, turns), lambda i: (0, i, 0)),
    )
    filter_grad, projected_grad = pl.pallas_call(
        hand_over,
        out_shape=(
            jax.ShapeDtypeStruct((channels, turns), BF16),
            jax.ShapeDtypeStruct((3, channels, turns), BF16),
        ),
        grid=(4,),
        in_specs=blocks,
        out_specs=blocks,
        compiler_params=pltpu.CompilerParams(vmem_limit_bytes=56 << 20),
    )(filter_grad, projected_grad)
    return (
        filter_grad.reshape(channels, 1, 1, turns),
        projected_grad.reshape(3, channels, 1, 1, turns),
    )


def solution(mesh):
    in_specs = (
        P(None, None, "row", "col", None),
        P(),
        P(None, "row", "col", None),
        P(),
        P(None, "row", "col", None),
    )
    out_specs = (P(None, "row", "col", None), P(None, None, "row", "col", None))
    return jax.shard_map(
        on_device, mesh=mesh, in_specs=in_specs, out_specs=out_specs, check_vma=False
    )
```

```python
import functools
import math

import jax
import jax.numpy as jnp
import numpy as np
from jax import lax
from jax.experimental import pallas as pl
from jax.experimental.pallas import tpu as pltpu
from jax.sharding import PartitionSpec as P

MESH = pl.DeviceIdType.MESH
BF16 = jnp.bfloat16
F32 = jnp.float32
PAD = 80


def two(table):
    high = table.astype(np.float32).astype(BF16)
    low = (table - high.astype(np.float64)).astype(np.float32).astype(BF16)
    return np.stack([high, low])


def tables(turns, planes, depth):
    slots = planes * depth
    length = turns * slots
    half = turns // 2 + 1
    z, g = np.meshgrid(np.arange(depth), np.arange(planes), indexing="ij")
    r = ((g // 2) * 2 * depth + z * 2 + g % 2).reshape(-1)
    k = np.arange(half)
    angles = 2.0 * math.pi * (np.outer(k, np.arange(turns)) % turns) / turns
    weight = np.where((k == 0) | (k == turns // 2), 1.0, 2.0)[:, None]
    scale = 1.0 / length * length**-0.5

    def padded(table):
        return np.pad(table, [(0, PAD - half), (0, 0)])

    cosine, sine = padded(np.cos(angles)), padded(np.sin(angles))
    first = np.concatenate([cosine, -sine])
    weight = padded(weight) * scale
    last = np.concatenate([weight * cosine, weight * sine]).T
    angles = 2.0 * math.pi * np.outer(k, r) / length
    twist = np.stack([padded(np.cos(angles)), padded(np.sin(angles))]).astype(np.float32)
    angles = 2.0 * math.pi * (np.outer(r, r) % slots) / slots
    cosine, sine = np.cos(angles), np.sin(angles)
    block = np.block([[cosine, -sine], [sine, cosine]])
    return two(first), two(last), twist, two(block)


def split(values):
    high = values.astype(BF16)
    return high, (values - high.astype(F32)).astype(BF16)


def dot(left, right):
    return jnp.dot(left, right, preferred_element_type=F32)


def dot_t(left, right):
    return lax.dot_general(left, right, (((1,), (1,)), ((), ())), preferred_element_type=F32)


def kernel(
    planes,
    depth,
    taps_hbm,
    gains_hbm,
    projected,
    filt,
    cotangent,
    first_hbm,
    last_hbm,
    twist_hbm,
    block_hbm,
    filter_out,
    projected_out,
    raw,
    raw_near,
    filter_in,
    products,
    kept,
    own_in,
    leaving_in,
    arrived_in,
    own_out,
    leaving_out,
    arrived_out,
    returned,
    grads,
    grads_near,
    result,
    columns_of,
    whole_held,
    whole_in,
    whole_leaving_in,
    whole_arrived_in,
    whole_out,
    whole_leaving_out,
    whole_arrived_out,
    whole_returned,
    lines,
    taps,
    gains,
    first,
    last,
    twist,
    block,
    flat,
    spectra,
    factors,
    load_sem,
    table_sem,
    send_sem,
    recv_sem,
    halo_send,
    halo_recv,
    out_sem,
):
    chunks = filter_in.shape[0]
    turns = filter_in.shape[-1]
    slots = planes * depth
    half = slots // 2
    rows_all = planes // 2
    row = lax.axis_index("row")
    col = lax.axis_index("col")
    z = col // 2
    y = lax.rem(col, 2)
    g = row * 2 + y
    rank = row * 2 * depth + col

    def at_plane(step):
        peer = lax.rem(g + step + 1, planes)
        return peer, (peer // 2, z * 2 + lax.rem(peer, 2))

    def at_depth(step):
        away = (1 - 2 * lax.rem(step, 2)) * (step // 2 + 1)
        peer = lax.rem(z + away + depth, depth)
        return peer, (row, peer * 2 + y)

    up, down = z + 1, z + depth - 1
    two_later = (lax.rem(row + up // depth, rows_all), lax.rem(up, depth) * 2 + y)
    two_earlier = (
        lax.rem(row + rows_all - 1 + down // depth, rows_all),
        lax.rem(down, depth) * 2 + y,
    )
    partner = (row, z * 2 + 1 - y)
    sides = (pl.ds(0, half), pl.ds(half, half))

    def await_bytes(ref, sem):
        pltpu.make_async_copy(ref, ref, sem).wait()

    early, middle = 1, 2
    whole = chunks * slots

    def load_whole():
        rows = pl.ds(whole, slots)
        return (
            pltpu.make_async_copy(
                projected.at[:, rows], whole_held.at[0, pl.ds(0, 3)], load_sem.at[chunks, 0]
            ),
            pltpu.make_async_copy(filt.at[rows], whole_held.at[0, 3], load_sem.at[chunks, 1]),
            pltpu.make_async_copy(
                cotangent.at[rows], whole_held.at[0, 4], load_sem.at[chunks, 2]
            ),
        )

    def whole_copies():
        rows = pl.ds(whole, slots)
        return (
            pltpu.make_async_copy(
                whole_returned.at[0, pl.ds(0, 3)],
                projected_out.at[:, rows],
                out_sem.at[chunks, 0],
            ),
            pltpu.make_async_copy(
                whole_returned.at[0, 3], filter_out.at[rows], out_sem.at[chunks, 1]
            ),
        )

    def load_copies(j):
        rows = pl.ds(j * slots, slots)
        return (
            pltpu.make_async_copy(
                projected.at[:, rows], raw.at[j, 0, pl.ds(0, 3)], load_sem.at[j, 0]
            ),
            pltpu.make_async_copy(cotangent.at[rows], raw.at[j, 0, 3], load_sem.at[j, 1]),
            pltpu.make_async_copy(filt.at[rows], filter_in.at[j], load_sem.at[j, 2]),
        )

    def table_copies():
        pairs = (
            (taps_hbm, taps),
            (gains_hbm, gains),
            (first_hbm, first),
            (last_hbm, last),
            (twist_hbm, twist),
            (block_hbm, block),
        )
        return [
            pltpu.make_async_copy(source, target, table_sem.at[i])
            for i, (source, target) in enumerate(pairs)
        ]

    def out_copies(j):
        rows = pl.ds(j * slots, slots)
        return (
            pltpu.make_async_copy(result.at[j], projected_out.at[:, rows], out_sem.at[j, 0]),
            pltpu.make_async_copy(returned.at[j, 2], filter_out.at[rows], out_sem.at[j, 1]),
        )

    def halo(kind, j, source, target, device):
        return pltpu.make_async_remote_copy(
            src_ref=source,
            dst_ref=target,
            send_sem=halo_send.at[kind, j],
            recv_sem=halo_recv.at[kind, j],
            device_id=device,
            device_id_type=MESH,
        )

    def far_halo(way, side, j):
        arrays = pl.ds(0, 4 if (way, side) == (0, 1) else 3)
        held = (raw, grads)[way]
        return halo(
            way * 2 + side,
            j,
            held.at[j, 0, arrays, sides[side]],
            held.at[j, 1, arrays, sides[side]],
            two_later if way == side else two_earlier,
        )

    def near_halo(way, side, j):
        held, near = ((raw, raw_near), (grads, grads_near))[way]
        own_or_far = y if way == side else 1 - y
        return halo(
            4 + way * 2 + side,
            j,
            held.at[j, own_or_far, pl.ds(0, 3), sides[side]],
            near.at[j, :, sides[side]],
            partner,
        )

    def loop(count, body):
        lax.fori_loop(0, count, lambda i, carry: (body(i), carry)[1], 0)

    for j in range(chunks):
        for copy in load_copies(j):
            copy.start()
    for copy in load_whole():
        copy.start()
    for copy in table_copies():
        copy.start()

    barrier = pltpu.get_barrier_semaphore()

    def greet(at):
        def one(i):
            _, device = at(i)
            pl.semaphore_signal(barrier, inc=1, device_id=device, device_id_type=MESH)

        return one

    loop(depth - 1, greet(at_depth))
    loop(planes - 1, greet(at_plane))
    for device in (two_later, two_earlier):
        pl.semaphore_signal(barrier, inc=1, device_id=device, device_id_type=MESH)
    pl.semaphore_wait(barrier, planes + depth)

    def send_all(phase, j, source, target, start=0, stop=None):
        count, at, own = (planes, at_plane, g) if phase in (2, 3, 6, 7) else (depth, at_depth, z)
        stop = count - 1 if stop is None else stop
        if start == 0:
            pltpu.make_async_copy(source(own), target(own), recv_sem.at[phase, j]).start()

        def one(i):
            peer, device = at(i)
            pltpu.make_async_remote_copy(
                src_ref=source(peer),
                dst_ref=target(own),
                send_sem=send_sem.at[phase, j],
                recv_sem=recv_sem.at[phase, j],
                device_id=device,
                device_id_type=MESH,
            ).start()

        lax.fori_loop(start, stop, lambda i, carry: (one(i), carry)[1], 0)

    def exchange(source, target, j):
        outer, arrays, inner = source.shape[1:4]

        def one(i):
            flat[...] = source[j, :, i].astype(F32).reshape(slots, turns)
            for k in range(inner):
                target[j, k, i] = flat[pl.ds(k, outer, stride=inner), :].astype(BF16)

        loop(arrays, one)

    def part(peer):
        return pl.ds(pl.multiple_of(peer * planes, planes), planes)

    def enter(j):
        for copy in load_copies(j):
            copy.wait()
        for side in range(2):
            far_halo(0, side, j).start()
        send_all(0, j, lambda peer: filter_in.at[j, part(peer)], lambda own: own_in.at[j, own, 0])

    loop(chunks, enter)
    for copy in load_whole():
        copy.wait()
    for copy in table_copies():
        copy.wait()

    def make_columns(j):
        mine = pl.ds(pl.multiple_of(j * slots, slots), slots)
        which = lax.broadcasted_iota(jnp.int32, (16, slots), 0)
        packed = jnp.where(which == 9, gains[:, mine], 0.0)
        for i in range(3):
            for t in range(3):
                packed = jnp.where(which == i * 3 + t, taps[i, pl.ds(t, 1), mine], packed)
        columns_of[j] = jnp.transpose(packed)

    loop(chunks, make_columns)

    lane = lax.broadcasted_iota(jnp.int32, (half, turns), 1)
    ranks = jnp.full((half, turns), rank, jnp.int32)
    final = lane == turns - 1
    last_two, last_one, next_last = ranks >= slots - 2, ranks == slots - 1, ranks == slots - 2
    first_two, first_one = ranks < 2, ranks == 0

    def wrap_back(values, where, fill):
        moved = pltpu.roll(values, 1, 1)
        if fill:
            moved = jnp.where(lane == 0, 0.0, moved)
        return jnp.where(where, moved, values)

    def wrap_ahead(values, where, fill):
        moved = pltpu.roll(values, turns - 1, 1)
        if fill:
            moved = jnp.where(final, 0.0, moved)
        return jnp.where(where, moved, values)

    def drop(values, where):
        return jnp.where(jnp.logical_and(final, where), 0.0, values)

    def column(j, side, k):
        return columns_of[j, sides[side], pl.ds(k, 1)]

    def filtered(j, side, i, lines):
        return (
            column(j, side, i * 3) * lines[0]
            + column(j, side, i * 3 + 1) * lines[1]
            + column(j, side, i * 3 + 2) * lines[2]
        )

    def pass_near(way):
        def one(j):
            for side in range(2):
                far_halo(way, side, j).wait_recv()
                near_halo(way, side, j).start()

        return one

    def make_products(j):
        for side in range(2):
            rows = sides[side]
            near_halo(0, side, j).wait_recv()

            def feature(i):
                own = raw[j, 0, i, rows].astype(F32)
                near = raw_near[j, i, rows].astype(F32)
                far = raw[j, 1, i, rows].astype(F32)
                if side == 0:
                    near = wrap_back(near, first_one, True)
                    far = wrap_back(far, first_two, True)
                    return filtered(j, side, i, (own, near, far))
                far = wrap_ahead(far, last_two, False)
                near = drop(wrap_ahead(near, last_one, False), next_last)
                return filtered(j, side, i, (far, near, drop(own, last_two)))

            if side == 0:
                seed = raw[j, 0, 3, rows].astype(F32)
            else:
                seed = wrap_ahead(raw[j, 1, 3, rows].astype(F32), last_two, False)
            kept[j, 3, rows] = seed
            weighted = feature(0) * seed
            kept[j, 2, rows] = weighted
            products[j, 1, rows] = weighted.astype(BF16)
            keys = feature(1)
            kept[j, 0, rows] = keys
            values = feature(2)
            kept[j, 1, rows] = values
            products[j, 0, rows] = (keys * values).astype(BF16)
        send_all(
            1,
            j,
            lambda peer: products.at[j, :, part(peer)],
            lambda own: own_in.at[j, own, pl.ds(1, 2)],
        )

    def products_in_turn(j):
        @pl.when(j + 1 < chunks)
        def _():
            pass_near(0)(j + 1)

        make_products(j)

    pass_near(0)(0)
    loop(chunks, products_in_turn)
    send_all(
        5,
        0,
        lambda peer: whole_held.at[0, :, part(peer)],
        lambda own: whole_in.at[0, own],
    )

    def transform():
        width = min(256, 2 * slots)

        def columns(i):
            at = pl.ds(pl.multiple_of(i * width, width), width)
            high, low = factors[0], factors[1]
            spectra[:, at] = dot(high, block[0, :, at]) + (
                dot(low, block[0, :, at]) + dot(high, block[1, :, at])
            )

        loop(2 * slots // width, columns)

    def put(i, real, imag):
        rows = pl.ds(i * PAD, PAD)
        for side, part in ((0, real), (slots, imag)):
            high, low = split(part)
            factors[0, rows, pl.ds(side, slots)] = high
            factors[1, rows, pl.ds(side, slots)] = low

    def get(i):
        rows = pl.ds(i * PAD, PAD)
        return spectra[rows, pl.ds(0, slots)], spectra[rows, pl.ds(slots, slots)]

    row_of = lax.broadcasted_iota(jnp.int32, (slots, turns), 0)
    odd = lax.rem(row_of, 2) == 1
    edge_row = lax.broadcasted_iota(jnp.int32, (planes, turns), 0)
    edge_lane = lax.broadcasted_iota(jnp.int32, (planes, turns), 1)

    def earlier(now):
        edge = pltpu.roll(now[slots - planes :], 2, 0)
        wrapped = jnp.where(edge_lane == 0, 0.0, pltpu.roll(edge, 1, 1))
        edge = jnp.where(edge_row < 2, wrapped, edge)
        second = jnp.concatenate([edge, now[: slots - planes]], axis=0)
        return jnp.where(odd, pltpu.roll(now, 1, 0), pltpu.roll(second, slots - 1, 0)), second

    def later(now):
        edge = pltpu.roll(now[:planes], planes - 2, 0)
        wrapped = jnp.where(edge_lane == turns - 1, 0.0, pltpu.roll(edge, turns - 1, 1))
        edge = jnp.where(edge_row >= planes - 2, wrapped, edge)
        second = jnp.concatenate([now[planes:], edge], axis=0)
        return jnp.where(odd, pltpu.roll(second, 1, 0), pltpu.roll(now, slots - 1, 0)), second

    def spectral(analyse, keep):
        for i in range(3):
            turned = analyse(i)
            real, imag = turned[:PAD], turned[PAD:]
            put(i, real * twist[0] + imag * twist[1], imag * twist[0] - real * twist[1])
        transform()
        filt_re, filt_im = get(0)
        gated_re, gated_im = get(1)
        put(
            0,
            gated_re * filt_re - gated_im * filt_im,
            -(gated_re * filt_im) - gated_im * filt_re,
        )
        side_re, side_im = get(2)
        put(
            1,
            side_re * filt_re + side_im * filt_im,
            side_re * filt_im - side_im * filt_re,
        )
        put(
            2,
            side_re * gated_re + side_im * gated_im,
            side_re * gated_im - side_im * gated_re,
        )
        transform()

        for i in range(3):
            real, imag = get(i)
            turned = jnp.concatenate(
                [real * twist[0] + imag * twist[1], imag * twist[0] - real * twist[1]], axis=0
            )
            high, low = split(turned)
            line = dot(last[0], high) + (dot(last[0], low) + dot(last[1], high))
            keep(i, jnp.transpose(line))

    def whole_gather():
        await_bytes(whole_in.at[0], recv_sem.at[5, 0])
        exchange(whole_in, whole_leaving_in, 0)
        send_all(
            6,
            0,
            lambda peer: whole_leaving_in.at[0, peer],
            lambda own: whole_arrived_in.at[0, own],
        )

    def whole_channel():
        await_bytes(whole_arrived_in.at[0], recv_sem.at[6, 0])
        exchange(whole_arrived_in, whole_in, 0)
        mine = pl.ds(whole, slots)
        here = lax.broadcasted_iota(jnp.int32, (1, slots), 1) == z * planes + g

        def pick(values):
            return jnp.sum(jnp.where(here, values, 0.0), axis=1, keepdims=True)

        tap = [[pick(taps[i, pl.ds(t, 1), mine]) for t in range(3)] for i in range(3)]
        gain = pick(gains[:, mine])

        def line(i):
            return whole_in[0, :, i].astype(F32).reshape(slots, turns)

        def feature(i):
            now = line(i)
            first_back, second_back = earlier(now)
            return tap[i][0] * now + tap[i][1] * first_back + tap[i][2] * second_back

        lines[0] = line(3)
        lines[3] = feature(1)
        lines[4] = feature(2)
        lines[1] = lines[3] * lines[4]
        lines[2] = feature(0) * line(4)

        def analyse(i):
            high, low = split(lines[i])
            return dot_t(first[0], high) + (dot_t(first[0], low) + dot_t(first[1], high))

        def keep(i, result_line):
            if i == 2:
                whole_out[0, :, 3] = result_line.astype(BF16).reshape(depth, planes, turns)
            else:
                lines[1 + i] = result_line + gain * lines[1 + i]

        spectral(analyse, keep)

        def leave(i, grad):
            now = grad.astype(BF16).astype(F32)
            first_next, second_next = later(now)
            total = tap[i][0] * now + tap[i][1] * first_next + tap[i][2] * second_next
            whole_out[0, :, i] = total.astype(BF16).reshape(depth, planes, turns)

        leave(0, line(4) * lines[1])
        leave(1, lines[2] * lines[4])
        leave(2, lines[2] * lines[3])
        exchange(whole_out, whole_leaving_out, 0)
        send_all(
            7,
            0,
            lambda peer: whole_leaving_out.at[0, peer],
            lambda own: whole_arrived_out.at[0, own],
        )

    def whole_scatter():
        await_bytes(whole_arrived_out.at[0], recv_sem.at[7, 0])
        exchange(whole_arrived_out, whole_out, 0)

    def whole_back(start, stop):
        send_all(
            8,
            0,
            lambda peer: whole_out.at[0, peer],
            lambda own: whole_returned.at[0, :, part(own)],
            start,
            stop,
        )

    def gather(j):
        await_bytes(own_in.at[j, :, 0], recv_sem.at[0, j])
        await_bytes(own_in.at[j, :, pl.ds(1, 2)], recv_sem.at[1, j])
        exchange(own_in, leaving_in, j)
        send_all(2, j, lambda peer: leaving_in.at[j, peer], lambda own: arrived_in.at[j, own])

    def own_channel(j):
        await_bytes(arrived_in.at[j], recv_sem.at[2, j])
        exchange(arrived_in, own_in, j)

        def analyse(i):
            line = own_in[j, :, i].reshape(slots, turns)
            return dot_t(first[0], line) + dot_t(first[1], line)

        def keep(i, line):
            own_out[j, :, i] = line.astype(BF16).reshape(depth, planes, turns)

        spectral(analyse, keep)
        exchange(own_out, leaving_out, j)
        send_all(3, j, lambda peer: leaving_out.at[j, peer], lambda own: arrived_out.at[j, own])

    def scatter(j):
        await_bytes(arrived_out.at[j], recv_sem.at[3, j])
        exchange(arrived_out, own_out, j)
        send_all(
            4, j, lambda peer: own_out.at[j, peer], lambda own: returned.at[j, :, part(own)]
        )

    def channel_in_turn(j):
        own_channel(j)

        @pl.when(j + 1 < chunks)
        def _():
            gather(j + 1)

        @pl.when(j + 1 == chunks)
        def _():
            whole_gather()

        scatter(j)

    gather(0)
    loop(chunks, channel_in_turn)
    whole_channel()
    whole_scatter()
    whole_back(0, early)

    def make_grads(j):
        await_bytes(returned.at[j], recv_sem.at[4, j])
        out_copies(j)[1].start()
        for side in range(2):
            rows = sides[side]
            gain = column(j, side, 9)
            keys, values = kept[j, 0, rows], kept[j, 1, rows]
            mixed = returned[j, 0, rows].astype(F32) + gain * (keys * values)
            grads[j, 0, 0, rows] = (kept[j, 3, rows] * mixed).astype(BF16)
            gated_grad = returned[j, 1, rows].astype(F32) + gain * kept[j, 2, rows]
            grads[j, 0, 1, rows] = (gated_grad * values).astype(BF16)
            grads[j, 0, 2, rows] = (gated_grad * keys).astype(BF16)
            far_halo(1, side, j).start()

    loop(chunks - 1, make_grads)
    whole_back(early, middle)
    make_grads(chunks - 1)
    whole_back(middle, depth - 1)
    loop(chunks, pass_near(1))

    def finish(j):
        for side in range(2):
            rows = sides[side]
            near_halo(1, side, j).wait_recv()
            for i in range(3):
                own = grads[j, 0, i, rows].astype(F32)
                near = grads_near[j, i, rows].astype(F32)
                far = grads[j, 1, i, rows].astype(F32)
                if side == 0:
                    near = wrap_ahead(near, last_one, True)
                    far = wrap_ahead(far, last_two, True)
                    total = filtered(j, side, i, (own, near, far))
                else:
                    far = wrap_back(far, first_two, False)
                    near = drop(wrap_back(near, first_one, False), last_one)
                    total = filtered(j, side, i, (far, near, drop(own, last_two)))
                result[j, i, rows] = total.astype(BF16)
        out_copies(j)[0].start()

    loop(chunks, finish)
    await_bytes(whole_returned.at[0], recv_sem.at[8, 0])
    for copy in whole_copies():
        copy.start()

    def close(j):
        for copy in out_copies(j):
            copy.wait()
        others = pl.ds(0, (depth - 1) * planes)
        await_bytes(filter_in.at[j, others], send_sem.at[0, j])
        await_bytes(products.at[j, :, others], send_sem.at[1, j])
        await_bytes(leaving_in.at[j, pl.ds(0, planes - 1)], send_sem.at[2, j])
        await_bytes(leaving_out.at[j, pl.ds(0, planes - 1)], send_sem.at[3, j])
        await_bytes(own_out.at[j, pl.ds(0, depth - 1)], send_sem.at[4, j])
        for way in range(2):
            for side in range(2):
                far_halo(way, side, j).wait_send()
                near_halo(way, side, j).wait_send()

    loop(chunks, close)
    for copy in whole_copies():
        copy.wait()
    await_bytes(whole_held.at[0, :, pl.ds(0, (depth - 1) * planes)], send_sem.at[5, 0])
    await_bytes(whole_leaving_in.at[0, pl.ds(0, planes - 1)], send_sem.at[6, 0])
    await_bytes(whole_leaving_out.at[0, pl.ds(0, planes - 1)], send_sem.at[7, 0])
    await_bytes(whole_out.at[0, pl.ds(0, depth - 1)], send_sem.at[8, 0])


def hand_over(filter_in, projected_in, filter_out, projected_out, passing, in_sem, out_sem):
    half = filter_in.shape[0] // 2
    copies = []
    for k in range(8):
        array, rows = k // 2, pl.ds(k % 2 * half, half)
        source = projected_in.at[array, rows] if array < 3 else filter_in.at[rows]
        target = projected_out.at[array, rows] if array < 3 else filter_out.at[rows]
        held = passing.at[array, rows]
        copies.append(
            (
                pltpu.make_async_copy(source, held, in_sem.at[k]),
                pltpu.make_async_copy(held, target, out_sem.at[k]),
            )
        )
    for first, _ in copies:
        first.start()
    for first, second in copies:
        first.wait()
        second.start()
    for _, second in copies:
        second.wait()


def on_device(projected, short_taps, long_filter, skip_gain, cotangent):
    channels = short_taps.shape[1]
    turns = projected.shape[-1]
    rows = lax.axis_size("row")
    depth = lax.axis_size("col") // 2
    planes = rows * 2
    slots = planes * depth
    chunks = channels // slots - 1
    made = [jnp.asarray(t) for t in tables(turns, planes, depth)]
    anywhere = pl.BlockSpec(memory_space=pl.ANY)

    def vmem(*shape, dtype=BF16):
        return pltpu.VMEM(shape, dtype)

    filter_grad, projected_grad = pl.pallas_call(
        functools.partial(kernel, planes, depth),
        out_shape=(
            jax.ShapeDtypeStruct((channels, turns), BF16),
            jax.ShapeDtypeStruct((3, channels, turns), BF16),
        ),
        in_specs=[anywhere] * 9,
        out_specs=(anywhere, anywhere),
        scratch_shapes=[
            vmem(chunks, 2, 4, slots, turns),
            vmem(chunks, 3, slots, turns),
            vmem(chunks, slots, turns),
            vmem(chunks, 2, slots, turns),
            vmem(chunks, 4, slots, turns, dtype=F32),
            vmem(chunks, depth, 3, planes, turns),
            vmem(chunks, planes, 3, depth, turns),
            vmem(chunks, planes, 3, depth, turns),
            vmem(chunks, depth, 3, planes, turns),
            vmem(chunks, planes, 3, depth, turns),
            vmem(chunks, planes, 3, depth, turns),
            vmem(chunks, 3, slots, turns),
            vmem(chunks, 2, 3, slots, turns),
            vmem(chunks, 3, slots, turns),
            vmem(chunks, 3, slots, turns),
            vmem(chunks, slots, 16, dtype=F32),
            vmem(1, 5, slots, turns),
            vmem(1, depth, 5, planes, turns),
            vmem(1, planes, 5, depth, turns),
            vmem(1, planes, 5, depth, turns),
            vmem(1, depth, 4, planes, turns),
            vmem(1, planes, 4, depth, turns),
            vmem(1, planes, 4, depth, turns),
            vmem(1, 4, slots, turns),
            vmem(5, slots, turns, dtype=F32),
            vmem(3, 3, channels, dtype=F32),
            vmem(1, channels, dtype=F32),
            *[pltpu.VMEM(t.shape, t.dtype) for t in made],
            vmem(slots, turns, dtype=F32),
            vmem(3 * PAD, 2 * slots, dtype=F32),
            vmem(2, 3 * PAD, 2 * slots),
            pltpu.SemaphoreType.DMA((chunks + 1, 3)),
            pltpu.SemaphoreType.DMA((6,)),
            pltpu.SemaphoreType.DMA((9, chunks)),
            pltpu.SemaphoreType.DMA((9, chunks)),
            pltpu.SemaphoreType.DMA((8, chunks)),
            pltpu.SemaphoreType.DMA((8, chunks)),
            pltpu.SemaphoreType.DMA((chunks + 1, 2)),
        ],
        compiler_params=pltpu.CompilerParams(
            collective_id=0, has_side_effects=True, vmem_limit_bytes=56 << 20
        ),
    )(
        jnp.swapaxes(short_taps, 1, 2),
        skip_gain.reshape(1, channels),
        projected.reshape(3, channels, turns),
        long_filter.reshape(channels, turns),
        cotangent.reshape(channels, turns),
        *made,
    )
    filter_grad, projected_grad = pl.pallas_call(
        hand_over,
        out_shape=(
            jax.ShapeDtypeStruct((channels, turns), BF16),
            jax.ShapeDtypeStruct((3, channels, turns), BF16),
        ),
        in_specs=[anywhere] * 2,
        out_specs=(anywhere, anywhere),
        scratch_shapes=[
            vmem(4, channels, turns),
            pltpu.SemaphoreType.DMA((8,)),
            pltpu.SemaphoreType.DMA((8,)),
        ],
        compiler_params=pltpu.CompilerParams(vmem_limit_bytes=56 << 20),
    )(filter_grad, projected_grad)
    return (
        filter_grad.reshape(channels, 1, 1, turns),
        projected_grad.reshape(3, channels, 1, 1, turns),
    )


def solution(mesh):
    in_specs = (
        P(None, None, "row", "col", None),
        P(),
        P(None, "row", "col", None),
        P(),
        P(None, "row", "col", None),
    )
    out_specs = (P(None, "row", "col", None), P(None, None, "row", "col", None))
    return jax.shard_map(
        on_device, mesh=mesh, in_specs=in_specs, out_specs=out_specs, check_vma=False
    )
```
